256 devices in a mesh: energy: 16 (over x_lo, y, core), tile: 16 (over x_hi, z).
Axes of the slice: x: 4 (x_hi: 2, x_lo: 2; x = x_hi * 2 + x_lo), y: 4, z: 8, core: 2. Of those that a mesh axis runs over, the one named last changes fastest.
Arguments:
- lesser: float32 [2, 512, 16, 4096], P(None, 'energy', 'tile'), may hold values from -6 to 6
- greater: float32 [2, 512, 16, 4096], P(None, 'energy', 'tile'), may hold values from -6 to 6
Outputs:
- polarization: float32 [2, 512, 16, 4096], P(None, 'energy', 'tile')
The draws below stay inside these ranges and needn't reach their ends.
All inputs are finite; a program needn't handle non-finite values.
Results may differ from the reference program's by a relative error of at most 0.000098.
Values sent between devices are 32-bit elements; how exact they have to be, the bound alone decides.
A program may use at most 64 MiB of HBM per device.

```python
import jax
import jax.numpy as jnp
from jax import lax

ENERGIES = 512
TILE_SIDE = 4
TILE_COUNT = 16
BLOCK_SIDE = 64
BLOCK_CELLS = 4096


def shard_levels(key, dims, cuts, smallest, largest):
    def one(dim, shards_of):
        heights = jax.random.uniform(jax.random.fold_in(jax.random.fold_in(key, 6), dim), (shards_of,), jnp.float32, smallest / len(cuts), largest / len(cuts))
        return jnp.repeat(jnp.exp(heights), dims[dim] // shards_of).reshape((-1,) + (1,) * (len(dims) - dim - 1))

    level = one(*cuts[0])
    for cut in cuts[1:]:
        level = level * one(*cut)
    return level


def gaussian(own_key, extent, scale, most, shards=(), held_as=jnp.bfloat16):
    entries = jax.random.normal(own_key, extent, jnp.float32) * scale
    if len(shards) > 0:
        entries = shard_levels(own_key, extent, shards, -0.22, 0.18) * entries
    return jnp.clip(entries, min=-most, max=most).astype(held_as)


def setup_inputs(seed: int = 0) -> dict:
    key_of = jax.random.split(jax.random.key(seed), 3)
    return {
        "lesser": gaussian(key_of[0], (2, ENERGIES, TILE_COUNT, BLOCK_CELLS), 1.0, 6.0, ((1, 16), (2, 16)), jnp.float32),
        "greater": gaussian(key_of[1], (2, ENERGIES, TILE_COUNT, BLOCK_CELLS), 1.0, 6.0, ((1, 16), (2, 16)), jnp.float32),
    }


def reference(lesser, greater):
    side = TILE_SIDE
    block = BLOCK_SIDE
    mirrored = greater.reshape(2, ENERGIES, side, side, block, block)
    mirrored = mirrored.transpose(0, 1, 3, 2, 5, 4).reshape(2, ENERGIES, TILE_COUNT, BLOCK_CELLS)
    length = 2 * ENERGIES

    def one_tile(pair):
        lesser_tile, greater_tile = pair
        lower = lesser_tile[0] + 1j * lesser_tile[1]
        upper = greater_tile[0] + 1j * greater_tile[1]
        front = jnp.fft.fft(lower, n=length, axis=0)
        other = jnp.fft.ifft(upper, n=length, axis=0) * length
        corr = jnp.fft.ifft(front * other, axis=0)[:ENERGIES]
        result = -1j * corr * (ENERGIES ** -0.5)
        return jnp.stack([jnp.real(result), jnp.imag(result)]).astype(lesser.dtype)

    outputs = lax.map(one_tile, (lesser.transpose(2, 0, 1, 3), mirrored.transpose(2, 0, 1, 3)))
    return outputs.transpose(1, 2, 0, 3)
```

```python
import functools
import math

import jax
import jax.numpy as jnp
import ml_dtypes
import numpy as np
from jax import lax
from jax.experimental import pallas as pl
from jax.experimental.pallas import tpu as pltpu
from jax.sharding import PartitionSpec as P

MESH = pl.DeviceIdType.MESH
BF = jnp.bfloat16
F32 = jnp.float32


def tables(energies, lanes):
    length = 2 * energies
    quarter = length // 4
    n = np.arange(quarter)
    angle = 2.0 * np.pi * (np.outer(n, n) % quarter) / quarter
    cos, sin = np.cos(angle), np.sin(angle)
    full = np.block([[cos, sin], [-sin, cos]]).astype(np.float32)
    high = full.astype(ml_dtypes.bfloat16)
    low = (full - high.astype(np.float32)).astype(ml_dtypes.bfloat16)
    rows = []
    for q in (1, 2, 3):
        turn = 2.0 * np.pi * ((n * q) % length) / length
        rows.append(np.stack([np.cos(turn), -np.sin(turn)]))
    twiddle = np.stack(rows).astype(np.float32)
    twiddle = np.ascontiguousarray(np.broadcast_to(twiddle[..., None], twiddle.shape + (lanes,)))
    return np.stack([high, low]), twiddle


def split(x):
    high = x.astype(BF)
    return high, (x - high.astype(F32)).astype(BF)


def body(
    n_energy, side, lesser, greater, dft_hbm, tw_hbm, out,
    g_in, stage, turned, mirror_out, l_buf, g_buf, p_buf, dft, tw, y_hi, y_lo, spec, v_hi, v_lo, back,
    in_sem, own_sem, l_send, g_send, p_send, l_recv, g_recv, p_recv,
):
    e = lax.axis_index("energy")
    t = lax.axis_index("tile")
    t2 = (t % side) * side + t // side
    off_diagonal = t2 != t
    local = g_in.shape[1]
    energies = n_energy * local
    half = energies // 2

    load_g = pltpu.make_async_copy(greater, g_in, in_sem.at[0])
    load_g.start()
    load_dft = pltpu.make_async_copy(dft_hbm, dft, in_sem.at[1])
    load_tw = pltpu.make_async_copy(tw_hbm, tw, in_sem.at[2])

    barrier = pltpu.get_barrier_semaphore()

    @pl.loop(1, n_energy)
    def _(m):
        pl.semaphore_signal(barrier, inc=1, device_id=((e + m) % n_energy, t), device_id_type=MESH)

    @pl.when(off_diagonal)
    def _():
        @pl.loop(0, n_energy)
        def _(m):
            pl.semaphore_signal(barrier, inc=1, device_id=((e + m) % n_energy, t2), device_id_type=MESH)

        pl.semaphore_wait(barrier, 2 * n_energy - 1)

    @pl.when(jnp.logical_not(off_diagonal))
    def _():
        pl.semaphore_wait(barrier, n_energy - 1)

    def l_copy(h, to, frm):
        return pltpu.make_async_remote_copy(
            src_ref=lesser.at[:, :, 2 * to + h],
            dst_ref=l_buf.at[h, :, pl.ds(pl.multiple_of(frm * local, local), local)],
            send_sem=l_send.at[h, to],
            recv_sem=l_recv.at[h, frm],
            device_id=(to, t),
            device_id_type=MESH,
        )

    def g_copy(h, to, frm):
        return pltpu.make_async_remote_copy(
            src_ref=mirror_out.at[:, :, 2 * to + h],
            dst_ref=g_buf.at[h, :, pl.ds(pl.multiple_of(frm * local, local), local)],
            send_sem=g_send.at[h, to],
            recv_sem=g_recv.at[h, frm],
            device_id=(to, t2),
            device_id_type=MESH,
        )

    def p_copy(h, to, frm):
        return pltpu.make_async_remote_copy(
            src_ref=p_buf.at[h, :, pl.ds(pl.multiple_of(to * local, local), local)],
            dst_ref=out.at[:, :, 2 * frm + h],
            send_sem=p_send.at[h, to],
            recv_sem=p_recv.at[h, frm],
            device_id=(to, t),
            device_id_type=MESH,
        )

    def l_own(h):
        return pltpu.make_async_copy(
            lesser.at[:, :, 2 * e + h], l_buf.at[h, :, pl.ds(pl.multiple_of(e * local, local), local)], l_recv.at[h, e]
        )

    def g_own(h):
        return pltpu.make_async_copy(
            mirror_out.at[:, :, 2 * e + h], g_buf.at[h, :, pl.ds(pl.multiple_of(e * local, local), local)], g_recv.at[h, e]
        )

    def p_own(h):
        return pltpu.make_async_copy(
            p_buf.at[h, :, pl.ds(pl.multiple_of(e * local, local), local)], out.at[:, :, 2 * e + h], p_recv.at[h, e]
        )

    def send_l(h):
        @pl.loop(1, n_energy)
        def _(m):
            l_copy(h, (e + m) % n_energy, e).start()

        l_own(h).start()

    def send_g(h):
        @pl.loop(1, n_energy)
        def _(m):
            g_copy(h, (e + m) % n_energy, e).start()

        @pl.when(off_diagonal)
        def _():
            g_copy(h, e, e).start()

        @pl.when(jnp.logical_not(off_diagonal))
        def _():
            g_own(h).start()

    send_l(0)
    load_g.wait()

    low_lanes = lax.broadcasted_iota(jnp.int32, (32, 128), 1) < 64

    @pl.loop(0, 2 * (local // 4))
    def _(step):
        p = step // (local // 4)
        e0 = (step % (local // 4)) * 4
        for q in range(2):
            one = g_in[p, e0 + 2 * q]
            two = g_in[p, e0 + 2 * q + 1]
            stage[pl.ds(64 * q, 32, stride=2), :] = jnp.where(low_lanes, one, pltpu.roll(two, 64, 1))
            stage[pl.ds(64 * q + 1, 32, stride=2), :] = jnp.where(low_lanes, pltpu.roll(one, 64, 1), two)
        turned[...] = stage[...].T
        for w in range(2):
            even = turned[pl.ds(64 * w, 32, stride=2), :]
            odd = turned[pl.ds(64 * w + 1, 32, stride=2), :]
            mirror_out[p, e0 + w] = jnp.where(low_lanes, even, pltpu.roll(odd, 64, 1))
            mirror_out[p, e0 + 2 + w] = jnp.where(low_lanes, pltpu.roll(even, 64, 1), odd)

    send_g(0)
    send_l(1)
    send_g(1)
    load_dft.start()
    load_tw.start()
    load_dft.wait()
    load_tw.wait()

    factor = 1.0 / (2 * energies * math.sqrt(energies))

    def put(column, re, im):
        hi, lo = split(re)
        y_hi[:half, column : column + 128] = hi
        y_lo[:half, column : column + 128] = lo
        hi, lo = split(im)
        y_hi[half:, column : column + 128] = hi
        y_lo[half:, column : column + 128] = lo

    def front(buf, h, base, sign):
        re0, re1 = buf[h, 0, :half], buf[h, 0, half:]
        im0, im1 = sign * buf[h, 1, :half], sign * buf[h, 1, half:]
        put(base, re0 + re1, im0 + im1)
        for q, re, im in (
            (1, re0 + im1, im0 - re1),
            (2, re0 - re1, im0 - im1),
            (3, re0 - im1, im0 + re1),
        ):
            c, s = tw[q - 1, 0], tw[q - 1, 1]
            put(base + 128 * q, re * c - im * s, re * s + im * c)

    def dots(hi, lo, columns):
        dot = functools.partial(jnp.dot, preferred_element_type=F32)
        return (
            dot(dft[0], hi[:, columns]) + dot(dft[0], lo[:, columns]) + dot(dft[1], hi[:, columns])
        )

    @pl.loop(0, 2)
    def _(h):
        @pl.loop(1, n_energy)
        def _(m):
            l_copy(h, e, (e + n_energy - m) % n_energy).wait_recv()

        l_own(h).wait()

        @pl.loop(0, n_energy)
        def _(m):
            frm = (e + n_energy - m) % n_energy
            pltpu.make_async_copy(
                mirror_out.at[:, :, 0], g_buf.at[h, :, pl.ds(pl.multiple_of(frm * local, local), local)], g_recv.at[h, frm]
            ).wait()

        front(l_buf, h, 0, 1.0)
        front(g_buf, h, 512, -1.0)
        for c in range(4):
            columns = slice(256 * c, 256 * c + 256)
            spec[:, columns] = dots(y_hi, y_lo, columns)
        for c in range(4):
            one, two = slice(128 * c, 128 * c + 128), slice(512 + 128 * c, 640 + 128 * c)
            ar, ai = spec[:half, one], spec[half:, one]
            br, bi = spec[:half, two], spec[half:, two]
            hi, lo = split(ar * br + ai * bi)
            v_hi[:half, one] = hi
            v_lo[:half, one] = lo
            hi, lo = split(ar * bi - ai * br)
            v_hi[half:, one] = hi
            v_lo[half:, one] = lo
        for c in range(2):
            columns = slice(256 * c, 256 * c + 256)
            back[:, columns] = dots(v_hi, v_lo, columns)
        terms = [(back[:half, :128], back[half:, :128])]
        for q in (1, 2, 3):
            re, im = back[:half, 128 * q : 128 * q + 128], back[half:, 128 * q : 128 * q + 128]
            c, s = tw[q - 1, 0], tw[q - 1, 1]
            terms.append((re * c - im * s, re * s + im * c))
        (r0, i0), (r1, i1), (r2, i2), (r3, i3) = terms
        p_buf[h, 0, :half] = (i0 + i1 + i2 + i3) * -factor
        p_buf[h, 1, :half] = (r0 + r1 + r2 + r3) * -factor
        p_buf[h, 0, half:] = (i0 - r1 - i2 + r3) * -factor
        p_buf[h, 1, half:] = (r0 + i1 - r2 - i3) * -factor

        @pl.loop(1, n_energy)
        def _(m):
            p_copy(h, (e + m) % n_energy, e).start()

        p_own(h).start()

    @pl.loop(0, 2)
    def _(h):
        @pl.loop(1, n_energy)
        def _(m):
            to = (e + m) % n_energy
            l_copy(h, to, e).wait_send()
            g_copy(h, to, e).wait_send()
            p_copy(h, to, e).wait_send()
            p_copy(h, e, to).wait_recv()

        p_own(h).wait()

        @pl.when(off_diagonal)
        def _():
            g_copy(h, e, e).wait_send()


def on_device(lesser, greater):
    n_energy = lax.axis_size("energy")
    side = math.isqrt(lax.axis_size("tile"))
    local, cells = lesser.shape[1], lesser.shape[3]
    rows = cells // 128
    energies = n_energy * local
    dft, twiddle = tables(energies, 128)
    any_space = pl.BlockSpec(memory_space=pltpu.HBM)
    half = energies // 2
    out = pl.pallas_call(
        functools.partial(body, n_energy, side),
        out_shape=jax.ShapeDtypeStruct((2, local, rows, 128), F32),
        in_specs=[any_space] * 4,
        out_specs=any_space,
        scratch_shapes=[
            pltpu.VMEM((2, local, rows, 128), F32),
            pltpu.VMEM((128, 128), F32),
            pltpu.VMEM((128, 128), F32),
            pltpu.VMEM((2, local, rows, 128), F32),
            pltpu.VMEM((2, 2, energies, 128), F32),
            pltpu.VMEM((2, 2, energies, 128), F32),
            pltpu.VMEM((2, 2, energies, 128), F32),
            pltpu.VMEM((2, energies, energies), BF),
            pltpu.VMEM((3, 2, half, 128), F32),
            pltpu.VMEM((energies, 1024), BF),
            pltpu.VMEM((energies, 1024), BF),
            pltpu.VMEM((energies, 1024), F32),
            pltpu.VMEM((energies, 512), BF),
            pltpu.VMEM((energies, 512), BF),
            pltpu.VMEM((energies, 512), F32),
            pltpu.SemaphoreType.DMA((3,)),
            pltpu.SemaphoreType.DMA((2,)),
        ]
        + [pltpu.SemaphoreType.DMA((2, n_energy))] * 6,
        compiler_params=pltpu.CompilerParams(
            collective_id=0, has_side_effects=True, vmem_limit_bytes=40 * 2**20
        ),
        name="correlate",
    )(
        lesser.reshape(2, local, rows, 128),
        greater.reshape(2, local, rows, 128),
        jnp.asarray(dft),
        jnp.asarray(twiddle),
    )
    return out.reshape(2, local, 1, cells)


def solution(mesh):
    return jax.shard_map(
        on_device,
        mesh=mesh,
        in_specs=(P(None, "energy", "tile", None), P(None, "energy", "tile", None)),
        out_specs=P(None, "energy", "tile", None),
        check_vma=False,
    )
```

```python
import functools
import math

import jax
import jax.numpy as jnp
import ml_dtypes
import numpy as np
from jax import lax
from jax.experimental import pallas as pl
from jax.experimental.pallas import tpu as pltpu
from jax.sharding import PartitionSpec as P

MESH = pl.DeviceIdType.MESH
BF = jnp.bfloat16
F32 = jnp.float32


def tables(energies, lanes):
    length = 2 * energies
    quarter = length // 4
    n = np.arange(quarter)
    angle = 2.0 * np.pi * (np.outer(n, n) % quarter) / quarter
    cos, sin = np.cos(angle), np.sin(angle)
    full = np.block([[cos, sin], [-sin, cos]]).astype(np.float32)
    high = full.astype(ml_dtypes.bfloat16)
    low = (full - high.astype(np.float32)).astype(ml_dtypes.bfloat16)
    rows = []
    for q in (1, 2, 3):
        turn = 2.0 * np.pi * ((n * q) % length) / length
        rows.append(np.stack([np.cos(turn), -np.sin(turn)]))
    twiddle = np.stack(rows).astype(np.float32)
    twiddle = np.ascontiguousarray(np.broadcast_to(twiddle[..., None], twiddle.shape + (lanes,)))
    return np.stack([high, low]), twiddle


def split(x):
    high = x.astype(BF)
    return high, (x - high.astype(F32)).astype(BF)


def body(
    n_energy, side, lesser, greater, dft_hbm, tw_hbm, out,
    g_in, stage, turned, mirror_out, l_buf, g_buf, p_buf, held, dft, tw, y_hi, y_lo, spec, v_hi, v_lo, back,
    in_sem, own_sem, l_send, g_send, p_send, l_recv, g_recv, p_recv, r_recv, f_send,
):
    e = lax.axis_index("energy")
    t = lax.axis_index("tile")
    t2 = (t % side) * side + t // side
    off_diagonal = t2 != t
    local = g_in.shape[1]
    energies = n_energy * local
    half = energies // 2

    load_g = pltpu.make_async_copy(greater, g_in, in_sem.at[0])
    load_g.start()
    load_dft = pltpu.make_async_copy(dft_hbm, dft, in_sem.at[1])
    load_tw = pltpu.make_async_copy(tw_hbm, tw, in_sem.at[2])

    mirror = lambda k: (k % side) * side + k // side
    n_tile = side * side
    group = n_energy // 2
    base = (e // group) * group
    across = lambda k: (k + n_tile // 2) % n_tile
    crosses = lambda k: mirror(k) // (n_tile // 2) != k // (n_tile // 2)
    cross = crosses(t)
    relay = across(t)
    hands = crosses(relay)
    final = mirror(relay)
    last = across(t2)
    plain = jnp.logical_and(off_diagonal, jnp.logical_not(cross))

    barrier = pltpu.get_barrier_semaphore()

    def greet(to, tile):
        pl.semaphore_signal(barrier, inc=1, device_id=(to, tile), device_id_type=MESH)

    @pl.loop(1, n_energy)
    def _(m):
        greet((e + m) % n_energy, t)

    @pl.when(plain)
    def _():
        @pl.loop(0, n_energy)
        def _(m):
            greet((e + m) % n_energy, t2)

    @pl.when(cross)
    def _():
        greet(e, relay)

        @pl.loop(0, group)
        def _(m):
            greet((base + group + m) % n_energy, t2)
            greet(base + m, last)

    @pl.when(hands)
    def _():
        greet(e, relay)

        @pl.loop(0, group)
        def _(m):
            greet(base + m, final)

    def l_copy(h, to, frm):
        return pltpu.make_async_remote_copy(
            src_ref=lesser.at[:, :, h * n_energy + to],
            dst_ref=l_buf.at[h, :, pl.ds(pl.multiple_of(frm * local, local), local)],
            send_sem=l_send.at[h, to],
            recv_sem=l_recv.at[h, frm],
            device_id=(to, t),
            device_id_type=MESH,
        )

    def g_copy(h, to, frm):
        return pltpu.make_async_remote_copy(
            src_ref=mirror_out.at[:, :, h * n_energy + to],
            dst_ref=g_buf.at[h, :, pl.ds(pl.multiple_of(frm * local, local), local)],
            send_sem=g_send.at[h, to],
            recv_sem=g_recv.at[h, frm],
            device_id=(to, t2),
            device_id_type=MESH,
        )

    def first_leg(h, m):
        to = base + m
        return pltpu.make_async_remote_copy(
            src_ref=mirror_out.at[:, :, h * n_energy + to],
            dst_ref=held.at[h, m],
            send_sem=g_send.at[h, to],
            recv_sem=r_recv.at[h, m],
            device_id=(e, relay),
            device_id_type=MESH,
        )

    def second_leg(h, m):
        return pltpu.make_async_remote_copy(
            src_ref=held.at[h, m],
            dst_ref=g_buf.at[h, :, pl.ds(pl.multiple_of(e * local, local), local)],
            send_sem=f_send.at[h, m],
            recv_sem=g_recv.at[h, e],
            device_id=(base + m, final),
            device_id_type=MESH,
        )

    def p_copy(h, to, frm):
        return pltpu.make_async_remote_copy(
            src_ref=p_buf.at[h, :, pl.ds(pl.multiple_of(to * local, local), local)],
            dst_ref=out.at[:, :, h * n_energy + frm],
            send_sem=p_send.at[h, to],
            recv_sem=p_recv.at[h, frm],
            device_id=(to, t),
            device_id_type=MESH,
        )

    def l_own(h):
        return pltpu.make_async_copy(
            lesser.at[:, :, h * n_energy + e], l_buf.at[h, :, pl.ds(pl.multiple_of(e * local, local), local)], l_recv.at[h, e]
        )

    def g_own(h):
        return pltpu.make_async_copy(
            mirror_out.at[:, :, h * n_energy + e], g_buf.at[h, :, pl.ds(pl.multiple_of(e * local, local), local)], g_recv.at[h, e]
        )

    def p_own(h):
        return pltpu.make_async_copy(
            p_buf.at[h, :, pl.ds(pl.multiple_of(e * local, local), local)], out.at[:, :, h * n_energy + e], p_recv.at[h, e]
        )

    def send_l(h):
        @pl.loop(1, n_energy)
        def _(m):
            l_copy(h, (e + m) % n_energy, e).start()

        l_own(h).start()

    def send_g(h):
        @pl.when(cross)
        def _():
            @pl.loop(0, group)
            def _(m):
                k = (e + m) % group
                first_leg(h, k).start()
                g_copy(h, (base + group) % n_energy + k, e).start()

        @pl.when(jnp.logical_not(cross))
        def _():
            @pl.loop(1, n_energy)
            def _(m):
                g_copy(h, (e + m) % n_energy, e).start()

            @pl.when(off_diagonal)
            def _():
                g_copy(h, e, e).start()

            @pl.when(jnp.logical_not(off_diagonal))
            def _():
                g_own(h).start()

    def hand_on(h):
        @pl.when(hands)
        def _():
            @pl.loop(0, group)
            def _(m):
                k = (e + m) % group
                first_leg(h, k).wait_recv()
                second_leg(h, k).start()

    load_dft.start()
    load_tw.start()
    load_g.wait()

    low_lanes = lax.broadcasted_iota(jnp.int32, (32, 128), 1) < 64

    groups = stage.shape[0]

    @pl.loop(0, 2 * local // (4 * groups))
    def _(step):
        for k in range(groups):
            item = step * groups + k
            p = item // (local // 4)
            e0 = (item % (local // 4)) * 4
            for q in range(2):
                one = g_in[p, e0 + 2 * q]
                two = g_in[p, e0 + 2 * q + 1]
                stage[k, pl.ds(64 * q, 32, stride=2), :] = jnp.where(low_lanes, one, pltpu.roll(two, 64, 1))
                stage[k, pl.ds(64 * q + 1, 32, stride=2), :] = jnp.where(low_lanes, pltpu.roll(one, 64, 1), two)
        for k in range(groups):
            turned[k] = stage[k].T
        for k in range(groups):
            item = step * groups + k
            p = item // (local // 4)
            e0 = (item % (local // 4)) * 4
            for w in range(2):
                even = turned[k, pl.ds(64 * w, 32, stride=2), :]
                odd = turned[k, pl.ds(64 * w + 1, 32, stride=2), :]
                mirror_out[p, e0 + w] = jnp.where(low_lanes, even, pltpu.roll(odd, 64, 1))
                mirror_out[p, e0 + 2 + w] = jnp.where(low_lanes, pltpu.roll(even, 64, 1), odd)

    factor = 1.0 / (2 * energies * math.sqrt(energies))

    def put(column, re, im):
        hi, lo = split(re)
        y_hi[:half, column : column + 128] = hi
        y_lo[:half, column : column + 128] = lo
        hi, lo = split(im)
        y_hi[half:, column : column + 128] = hi
        y_lo[half:, column : column + 128] = lo

    def front(buf, h, base, sign):
        re0, re1 = buf[h, 0, :half], buf[h, 0, half:]
        im0, im1 = sign * buf[h, 1, :half], sign * buf[h, 1, half:]
        put(base, re0 + re1, im0 + im1)
        for q, re, im in (
            (1, re0 + im1, im0 - re1),
            (2, re0 - re1, im0 - im1),
            (3, re0 - im1, im0 + re1),
        ):
            c, s = tw[q - 1, 0], tw[q - 1, 1]
            put(base + 128 * q, re * c - im * s, re * s + im * c)

    def dots(rows, hi, lo, columns):
        dot = functools.partial(jnp.dot, preferred_element_type=F32)
        high, low = dft[0, rows], dft[1, rows]
        return dot(high, hi[:, columns]) + dot(high, lo[:, columns]) + dot(low, hi[:, columns])

    def wait_l(h):
        @pl.loop(1, n_energy)
        def _(m):
            l_copy(h, e, (e + n_energy - m) % n_energy).wait_recv()

        l_own(h).wait()

    def wait_g(h):
        @pl.loop(0, n_energy)
        def _(m):
            frm = (e + n_energy - m) % n_energy
            pltpu.make_async_copy(
                mirror_out.at[:, :, 0], g_buf.at[h, :, pl.ds(pl.multiple_of(frm * local, local), local)], g_recv.at[h, frm]
            ).wait()

    def compute_l(h):
        front(l_buf, h, 0, 1.0)
        for c in range(2):
            columns = slice(256 * c, 256 * c + 256)
            spec[:, columns] = dots(slice(None), y_hi, y_lo, columns)

    def compute_g(h):
        front(g_buf, h, 512, -1.0)
        for c in range(2, 4):
            columns = slice(256 * c, 256 * c + 256)
            spec[:, columns] = dots(slice(None), y_hi, y_lo, columns)
        for c in range(4):
            one, two = slice(128 * c, 128 * c + 128), slice(512 + 128 * c, 640 + 128 * c)
            ar, ai = spec[:half, one], spec[half:, one]
            br, bi = spec[:half, two], spec[half:, two]
            hi, lo = split(ar * br + ai * bi)
            v_hi[:half, one] = hi
            v_lo[:half, one] = lo
            hi, lo = split(ar * bi - ai * br)
            v_hi[half:, one] = hi
            v_lo[half:, one] = lo

    def finish(h, part):
        count = half // 2
        low, high = slice(count * part, count * part + count), slice(half + count * part, half + count * part + count)
        for c in range(2):
            columns = slice(256 * c, 256 * c + 256)
            back[low, columns] = dots(low, v_hi, v_lo, columns)
            back[high, columns] = dots(high, v_hi, v_lo, columns)
        terms = [(back[low, :128], back[high, :128])]
        for q in (1, 2, 3):
            re, im = back[low, 128 * q : 128 * q + 128], back[high, 128 * q : 128 * q + 128]
            c, s = tw[q - 1, 0, low], tw[q - 1, 1, low]
            terms.append((re * c - im * s, re * s + im * c))
        (r0, i0), (r1, i1), (r2, i2), (r3, i3) = terms
        p_buf[h, 0, low] = (i0 + i1 + i2 + i3) * -factor
        p_buf[h, 1, low] = (r0 + r1 + r2 + r3) * -factor
        p_buf[h, 0, high] = (i0 - r1 - i2 + r3) * -factor
        p_buf[h, 1, high] = (r0 + i1 - r2 - i3) * -factor

    def send_p(h, part):
        @pl.loop(0, n_energy // 2)
        def _(m):
            turn = (e + m) % (n_energy // 2)
            to = (turn // (n_energy // 4)) * group + part * (n_energy // 4) + turn % (n_energy // 4)

            @pl.when(to != e)
            def _():
                p_copy(h, to, e).start()

            @pl.when(to == e)
            def _():
                p_own(h).start()

    def drain_l(h):
        @pl.loop(1, n_energy)
        def _(m):
            l_copy(h, (e + m) % n_energy, e).wait_send()

    def drain_g(h):
        @pl.loop(1, n_energy)
        def _(m):
            g_copy(h, (e + m) % n_energy, e).wait_send()

        @pl.when(off_diagonal)
        def _():
            g_copy(h, e, e).wait_send()

        @pl.when(hands)
        def _():
            @pl.loop(0, group)
            def _(m):
                second_leg(h, m).wait_send()

    def drain_p(h):
        @pl.loop(1, n_energy)
        def _(m):
            to = (e + m) % n_energy
            p_copy(h, to, e).wait_send()
            p_copy(h, e, to).wait_recv()

        p_own(h).wait()

    signals = n_energy - 1 + jnp.where(plain, n_energy, 0)
    signals += jnp.where(cross, n_energy + 1, 0) + jnp.where(hands, group + 1, 0)
    pl.semaphore_wait(barrier, signals)

    send_g(0)
    send_l(0)
    send_g(1)
    send_l(1)
    hand_on(0)
    hand_on(1)
    load_dft.wait()
    load_tw.wait()

    @pl.loop(0, 2)
    def _(h):
        wait_l(h)
        compute_l(h)
        wait_g(h)
        compute_g(h)
        for part in range(2):
            finish(h, part)
            send_p(h, part)

    @pl.loop(0, 2)
    def _(h):
        drain_l(h)
        drain_g(h)
        drain_p(h)


def on_device(lesser, greater):
    n_energy = lax.axis_size("energy")
    side = math.isqrt(lax.axis_size("tile"))
    local, cells = lesser.shape[1], lesser.shape[3]
    rows = cells // 128
    energies = n_energy * local
    dft, twiddle = tables(energies, 128)
    any_space = pl.BlockSpec(memory_space=pltpu.HBM)
    half = energies // 2
    out = pl.pallas_call(
        functools.partial(body, n_energy, side),
        out_shape=jax.ShapeDtypeStruct((2, local, rows, 128), F32),
        in_specs=[any_space] * 4,
        out_specs=any_space,
        scratch_shapes=[
            pltpu.VMEM((2, local, rows, 128), F32),
            pltpu.VMEM((4, 128, 128), F32),
            pltpu.VMEM((4, 128, 128), F32),
            pltpu.VMEM((2, local, rows, 128), F32),
            pltpu.VMEM((2, 2, energies, 128), F32),
            pltpu.VMEM((2, 2, energies, 128), F32),
            pltpu.VMEM((2, 2, energies, 128), F32),
            pltpu.VMEM((2, n_energy // 2, 2, local, 128), F32),
            pltpu.VMEM((2, energies, energies), BF),
            pltpu.VMEM((3, 2, half, 128), F32),
            pltpu.VMEM((energies, 1024), BF),
            pltpu.VMEM((energies, 1024), BF),
            pltpu.VMEM((energies, 1024), F32),
            pltpu.VMEM((energies, 512), BF),
            pltpu.VMEM((energies, 512), BF),
            pltpu.VMEM((energies, 512), F32),
            pltpu.SemaphoreType.DMA((3,)),
            pltpu.SemaphoreType.DMA((2,)),
        ]
        + [pltpu.SemaphoreType.DMA((2, n_energy))] * 6
        + [pltpu.SemaphoreType.DMA((2, n_energy // 2))] * 2,
        compiler_params=pltpu.CompilerParams(
            collective_id=0, has_side_effects=True, vmem_limit_bytes=60 * 2**20
        ),
        name="correlate",
    )(
        lesser.reshape(2, local, rows, 128),
        greater.reshape(2, local, rows, 128),
        jnp.asarray(dft),
        jnp.asarray(twiddle),
    )
    return out.reshape(2, local, 1, cells)


def solution(mesh):
    return jax.shard_map(
        on_device,
        mesh=mesh,
        in_specs=(P(None, "energy", "tile", None), P(None, "energy", "tile", None)),
        out_specs=P(None, "energy", "tile", None),
        check_vma=False,
    )
```

```python
import functools
import math

import jax
import jax.numpy as jnp
import ml_dtypes
import numpy as np
from jax import lax
from jax.experimental import pallas as pl
from jax.experimental.pallas import tpu as pltpu
from jax.sharding import PartitionSpec as P

MESH = pl.DeviceIdType.MESH
BF = jnp.bfloat16
F32 = jnp.float32


def tables(energies, lanes):
    length = 2 * energies
    quarter = length // 4
    n = np.arange(quarter)
    angle = 2.0 * np.pi * (np.outer(n, n) % quarter) / quarter
    cos, sin = np.cos(angle), np.sin(angle)
    full = np.block([[cos, sin], [-sin, cos]]).astype(np.float32)
    high = full.astype(ml_dtypes.bfloat16)
    low = (full - high.astype(np.float32)).astype(ml_dtypes.bfloat16)
    rows = []
    for q in (1, 2, 3):
        turn = 2.0 * np.pi * ((n * q) % length) / length
        rows.append(np.stack([np.cos(turn), -np.sin(turn)]))
    twiddle = np.stack(rows).astype(np.float32)
    twiddle = np.ascontiguousarray(np.broadcast_to(twiddle[..., None], twiddle.shape + (lanes,)))
    return np.stack([high, low]), twiddle


def split(x):
    high = x.astype(BF)
    return high, (x - high.astype(F32)).astype(BF)


def body(
    n_energy, side, lesser, greater, dft_hbm, tw_hbm, out,
    g_in, stage, turned, mirror_out, l_buf, g_buf, p_buf, held, dft, tw, y_hi, y_lo, spec, v_hi, v_lo, back,
    in_sem, own_sem, l_send, g_send, p_send, l_recv, g_recv, p_recv, r_recv, f_send,
):
    e = lax.axis_index("energy")
    t = lax.axis_index("tile")
    t2 = (t % side) * side + t // side
    off_diagonal = t2 != t
    local = g_in.shape[1]
    energies = n_energy * local
    half = energies // 2

    load_g = pltpu.make_async_copy(greater, g_in, in_sem.at[0])
    load_g.start()
    load_dft = pltpu.make_async_copy(dft_hbm, dft, in_sem.at[1])
    load_tw = pltpu.make_async_copy(tw_hbm, tw, in_sem.at[2])

    mirror = lambda k: (k % side) * side + k // side
    n_tile = side * side
    group = n_energy // 2
    base = (e // group) * group
    across = lambda k: (k + n_tile // 2) % n_tile
    crosses = lambda k: mirror(k) // (n_tile // 2) != k // (n_tile // 2)
    cross = crosses(t)
    relay = across(t)
    hands = crosses(relay)
    final = mirror(relay)
    last = across(t2)
    plain = jnp.logical_and(off_diagonal, jnp.logical_not(cross))

    barrier = pltpu.get_barrier_semaphore()

    def greet(to, tile):
        pl.semaphore_signal(barrier, inc=1, device_id=(to, tile), device_id_type=MESH)

    @pl.loop(1, n_energy)
    def _(m):
        greet((e + m) % n_energy, t)

    @pl.when(plain)
    def _():
        @pl.loop(0, n_energy)
        def _(m):
            greet((e + m) % n_energy, t2)

    @pl.when(cross)
    def _():
        greet(e, relay)

        @pl.loop(0, group)
        def _(m):
            greet((base + group + m) % n_energy, t2)
            greet(base + m, last)

    @pl.when(hands)
    def _():
        greet(e, relay)

        @pl.loop(0, group)
        def _(m):
            greet(base + m, final)

    def l_copy(h, to, frm):
        return pltpu.make_async_remote_copy(
            src_ref=lesser.at[:, :, h * n_energy + to],
            dst_ref=l_buf.at[h, :, pl.ds(pl.multiple_of(frm * local, local), local)],
            send_sem=l_send.at[h, to],
            recv_sem=l_recv.at[h, frm],
            device_id=(to, t),
            device_id_type=MESH,
        )

    def g_copy(h, to, frm):
        return pltpu.make_async_remote_copy(
            src_ref=mirror_out.at[:, :, h * n_energy + to],
            dst_ref=g_buf.at[h, :, pl.ds(pl.multiple_of(frm * local, local), local)],
            send_sem=g_send.at[h, to],
            recv_sem=g_recv.at[h, frm],
            device_id=(to, t2),
            device_id_type=MESH,
        )

    def first_leg(h, m):
        to = base + m
        return pltpu.make_async_remote_copy(
            src_ref=mirror_out.at[:, :, h * n_energy + to],
            dst_ref=held.at[h, m],
            send_sem=g_send.at[h, to],
            recv_sem=r_recv.at[h, m],
            device_id=(e, relay),
            device_id_type=MESH,
        )

    def second_leg(h, m):
        return pltpu.make_async_remote_copy(
            src_ref=held.at[h, m],
            dst_ref=g_buf.at[h, :, pl.ds(pl.multiple_of(e * local, local), local)],
            send_sem=f_send.at[h, m],
            recv_sem=g_recv.at[h, e],
            device_id=(base + m, final),
            device_id_type=MESH,
        )

    def p_copy(h, to, frm):
        return pltpu.make_async_remote_copy(
            src_ref=p_buf.at[h, :, pl.ds(pl.multiple_of(to * local, local), local)],
            dst_ref=out.at[:, :, h * n_energy + frm],
            send_sem=p_send.at[h, to],
            recv_sem=p_recv.at[h, frm],
            device_id=(to, t),
            device_id_type=MESH,
        )

    def l_own(h):
        return pltpu.make_async_copy(
            lesser.at[:, :, h * n_energy + e], l_buf.at[h, :, pl.ds(pl.multiple_of(e * local, local), local)], l_recv.at[h, e]
        )

    def g_own(h):
        return pltpu.make_async_copy(
            mirror_out.at[:, :, h * n_energy + e], g_buf.at[h, :, pl.ds(pl.multiple_of(e * local, local), local)], g_recv.at[h, e]
        )

    def p_own(h):
        return pltpu.make_async_copy(
            p_buf.at[h, :, pl.ds(pl.multiple_of(e * local, local), local)], out.at[:, :, h * n_energy + e], p_recv.at[h, e]
        )

    def send_l(h):
        @pl.loop(1, n_energy)
        def _(m):
            l_copy(h, (e + m) % n_energy, e).start()

        l_own(h).start()

    def send_g(h):
        @pl.when(cross)
        def _():
            @pl.loop(0, group)
            def _(m):
                k = (e + m) % group
                first_leg(h, k).start()
                g_copy(h, (base + group) % n_energy + k, e).start()

        @pl.when(jnp.logical_not(cross))
        def _():
            @pl.loop(1, n_energy)
            def _(m):
                g_copy(h, (e + m) % n_energy, e).start()

            @pl.when(off_diagonal)
            def _():
                g_copy(h, e, e).start()

            @pl.when(jnp.logical_not(off_diagonal))
            def _():
                g_own(h).start()

    def hand_on(h):
        @pl.when(hands)
        def _():
            @pl.loop(0, group)
            def _(m):
                k = (e + m) % group
                first_leg(h, k).wait_recv()
                second_leg(h, k).start()

    load_dft.start()
    load_tw.start()
    load_g.wait()

    low_lanes = lax.broadcasted_iota(jnp.int32, (32, 128), 1) < 64

    groups = stage.shape[0]

    @pl.loop(0, 2 * local // (4 * groups))
    def _(step):
        for k in range(groups):
            item = step * groups + k
            p = item // (local // 4)
            e0 = (item % (local // 4)) * 4
            for q in range(2):
                one = g_in[p, e0 + 2 * q]
                two = g_in[p, e0 + 2 * q + 1]
                stage[k, pl.ds(64 * q, 32, stride=2), :] = jnp.where(low_lanes, one, pltpu.roll(two, 64, 1))
                stage[k, pl.ds(64 * q + 1, 32, stride=2), :] = jnp.where(low_lanes, pltpu.roll(one, 64, 1), two)
        for k in range(groups):
            turned[k] = stage[k].T
        for k in range(groups):
            item = step * groups + k
            p = item // (local // 4)
            e0 = (item % (local // 4)) * 4
            for w in range(2):
                even = turned[k, pl.ds(64 * w, 32, stride=2), :]
                odd = turned[k, pl.ds(64 * w + 1, 32, stride=2), :]
                mirror_out[p, e0 + w] = jnp.where(low_lanes, even, pltpu.roll(odd, 64, 1))
                mirror_out[p, e0 + 2 + w] = jnp.where(low_lanes, pltpu.roll(even, 64, 1), odd)

    factor = 1.0 / (2 * energies * math.sqrt(energies))

    def put(column, re, im):
        hi, lo = split(re)
        y_hi[:half, column : column + 128] = hi
        y_lo[:half, column : column + 128] = lo
        hi, lo = split(im)
        y_hi[half:, column : column + 128] = hi
        y_lo[half:, column : column + 128] = lo

    def front(buf, h, base, sign):
        re0, re1 = buf[h, 0, :half], buf[h, 0, half:]
        im0, im1 = sign * buf[h, 1, :half], sign * buf[h, 1, half:]
        put(base, re0 + re1, im0 + im1)
        for q, re, im in (
            (1, re0 + im1, im0 - re1),
            (2, re0 - re1, im0 - im1),
            (3, re0 - im1, im0 + re1),
        ):
            c, s = tw[q - 1, 0], tw[q - 1, 1]
            put(base + 128 * q, re * c - im * s, re * s + im * c)

    def dots(rows, hi, lo, columns):
        dot = functools.partial(jnp.dot, preferred_element_type=F32)
        high, low = dft[0, rows], dft[1, rows]
        return dot(high, hi[:, columns]) + dot(high, lo[:, columns]) + dot(low, hi[:, columns])

    def wait_l(h):
        @pl.loop(1, n_energy)
        def _(m):
            l_copy(h, e, (e + n_energy - m) % n_energy).wait_recv()

        l_own(h).wait()

    def wait_g(h):
        @pl.loop(0, n_energy)
        def _(m):
            frm = (e + n_energy - m) % n_energy
            pltpu.make_async_copy(
                mirror_out.at[:, :, 0], g_buf.at[h, :, pl.ds(pl.multiple_of(frm * local, local), local)], g_recv.at[h, frm]
            ).wait()

    def compute_l(h):
        front(l_buf, h, 0, 1.0)
        for c in range(2):
            columns = slice(256 * c, 256 * c + 256)
            spec[:, columns] = dots(slice(None), y_hi, y_lo, columns)

    def compute_g(h):
        front(g_buf, h, 512, -1.0)
        for c in range(2, 4):
            columns = slice(256 * c, 256 * c + 256)
            spec[:, columns] = dots(slice(None), y_hi, y_lo, columns)
        for c in range(4):
            one, two = slice(128 * c, 128 * c + 128), slice(512 + 128 * c, 640 + 128 * c)
            ar, ai = spec[:half, one], spec[half:, one]
            br, bi = spec[:half, two], spec[half:, two]
            hi, lo = split(ar * br + ai * bi)
            v_hi[:half, one] = hi
            v_lo[:half, one] = lo
            hi, lo = split(ar * bi - ai * br)
            v_hi[half:, one] = hi
            v_lo[half:, one] = lo

    def finish(h, part):
        count = half // 2
        low, high = slice(count * part, count * part + count), slice(half + count * part, half + count * part + count)
        for c in range(2):
            columns = slice(256 * c, 256 * c + 256)
            back[low, columns] = dots(low, v_hi, v_lo, columns)
            back[high, columns] = dots(high, v_hi, v_lo, columns)
        terms = [(back[low, :128], back[high, :128])]
        for q in (1, 2, 3):
            re, im = back[low, 128 * q : 128 * q + 128], back[high, 128 * q : 128 * q + 128]
            c, s = tw[q - 1, 0, low], tw[q - 1, 1, low]
            terms.append((re * c - im * s, re * s + im * c))
        (r0, i0), (r1, i1), (r2, i2), (r3, i3) = terms
        p_buf[h, 0, low] = (i0 + i1 + i2 + i3) * -factor
        p_buf[h, 1, low] = (r0 + r1 + r2 + r3) * -factor
        p_buf[h, 0, high] = (i0 - r1 - i2 + r3) * -factor
        p_buf[h, 1, high] = (r0 + i1 - r2 - i3) * -factor

    def send_p(h, part):
        @pl.loop(0, n_energy // 2)
        def _(m):
            turn = (e + m) % (n_energy // 2)
            to = (turn // (n_energy // 4)) * group + part * (n_energy // 4) + turn % (n_energy // 4)

            @pl.when(to != e)
            def _():
                p_copy(h, to, e).start()

            @pl.when(to == e)
            def _():
                p_own(h).start()

    def drain_l(h):
        @pl.loop(1, n_energy)
        def _(m):
            l_copy(h, (e + m) % n_energy, e).wait_send()

    def drain_g(h):
        @pl.loop(1, n_energy)
        def _(m):
            g_copy(h, (e + m) % n_energy, e).wait_send()

        @pl.when(off_diagonal)
        def _():
            g_copy(h, e, e).wait_send()

        @pl.when(hands)
        def _():
            @pl.loop(0, group)
            def _(m):
                second_leg(h, m).wait_send()

    def drain_p(h):
        @pl.loop(1, n_energy)
        def _(m):
            to = (e + m) % n_energy
            p_copy(h, to, e).wait_send()
            p_copy(h, e, to).wait_recv()

        p_own(h).wait()

    signals = n_energy - 1 + jnp.where(plain, n_energy, 0)
    signals += jnp.where(cross, n_energy + 1, 0) + jnp.where(hands, group + 1, 0)
    pl.semaphore_wait(barrier, signals)

    send_g(0)
    send_l(0)
    send_g(1)
    send_l(1)
    hand_on(0)
    hand_on(1)
    load_dft.wait()
    load_tw.wait()

    @pl.loop(0, 2)
    def _(h):
        wait_l(h)
        compute_l(h)
        wait_g(h)
        compute_g(h)
        for part in range(2):
            finish(h, part)
            send_p(h, part)

    @pl.loop(0, 2)
    def _(h):
        drain_l(h)
        drain_g(h)
        drain_p(h)


def on_device(lesser, greater):
    n_energy = lax.axis_size("energy")
    side = math.isqrt(lax.axis_size("tile"))
    local, cells = lesser.shape[1], lesser.shape[3]
    rows = cells // 128
    energies = n_energy * local
    dft, twiddle = tables(energies, 128)
    any_space = pl.BlockSpec(memory_space=pltpu.HBM)
    half = energies // 2
    out = pl.pallas_call(
        functools.partial(body, n_energy, side),
        out_shape=jax.ShapeDtypeStruct((2, local, rows, 128), F32),
        in_specs=[any_space] * 4,
        out_specs=any_space,
        scratch_shapes=[
            pltpu.VMEM((2, local, rows, 128), F32),
            pltpu.VMEM((4, 128, 128), F32),
            pltpu.VMEM((4, 128, 128), F32),
            pltpu.VMEM((2, local, rows, 128), F32),
            pltpu.VMEM((2, 2, energies, 128), F32),
            pltpu.VMEM((2, 2, energies, 128), F32),
            pltpu.VMEM((2, 2, energies, 128), F32),
            pltpu.VMEM((2, n_energy // 2, 2, local, 128), F32),
            pltpu.VMEM((2, energies, energies), BF),
            pltpu.VMEM((3, 2, half, 128), F32),
            pltpu.VMEM((energies, 1024), BF),
            pltpu.VMEM((energies, 1024), BF),
            pltpu.VMEM((energies, 1024), F32),
            pltpu.VMEM((energies, 512), BF),
            pltpu.VMEM((energies, 512), BF),
            pltpu.VMEM((energies, 512), F32),
            pltpu.SemaphoreType.DMA((3,)),
            pltpu.SemaphoreType.DMA((2,)),
        ]
        + [pltpu.SemaphoreType.DMA((2, n_energy))] * 6
        + [pltpu.SemaphoreType.DMA((2, n_energy // 2))] * 2,
        compiler_params=pltpu.CompilerParams(
            collective_id=0, has_side_effects=True, vmem_limit_bytes=40 * 2**20
        ),
        name="correlate",
    )(
        pltpu.with_memory_space_constraint(lesser.reshape(2, local, rows, 128), pltpu.HBM),
        pltpu.with_memory_space_constraint(greater.reshape(2, local, rows, 128), pltpu.HBM),
        pltpu.with_memory_space_constraint(jnp.asarray(dft), pltpu.HBM),
        pltpu.with_memory_space_constraint(jnp.asarray(twiddle), pltpu.HBM),
    )
    return out.reshape(2, local, 1, cells)


def solution(mesh):
    return jax.shard_map(
        on_device,
        mesh=mesh,
        in_specs=(P(None, "energy", "tile", None), P(None, "energy", "tile", None)),
        out_specs=P(None, "energy", "tile", None),
        check_vma=False,
    )
```

```python
import functools
import math

import jax
import jax.numpy as jnp
import ml_dtypes
import numpy as np
from jax import lax
from jax.experimental import pallas as pl
from jax.experimental.pallas import tpu as pltpu
from jax.sharding import PartitionSpec as P

MESH = pl.DeviceIdType.MESH
BF = jnp.bfloat16
F32 = jnp.float32


def tables(energies, lanes):
    length = 2 * energies
    quarter = length // 4
    n = np.arange(quarter)
    angle = 2.0 * np.pi * (np.outer(n, n) % quarter) / quarter
    cos, sin = np.cos(angle), np.sin(angle)
    full = np.block([[cos, sin], [-sin, cos]]).astype(np.float32)
    high = full.astype(ml_dtypes.bfloat16)
    low = (full - high.astype(np.float32)).astype(ml_dtypes.bfloat16)
    rows = []
    for q in (1, 2, 3):
        turn = 2.0 * np.pi * ((n * q) % length) / length
        rows.append(np.stack([np.cos(turn), -np.sin(turn)]))
    twiddle = np.stack(rows).astype(np.float32)
    twiddle = np.ascontiguousarray(np.broadcast_to(twiddle[..., None], twiddle.shape + (lanes,)))
    return np.stack([high, low]), twiddle


HALF, ROUND = 1, 2
KINDS = tuple((k, HALF) for k in (2, 3, 6, 7, 8, 9, 12, 13)) + tuple((k, ROUND) for k in (1, 4, 11, 14))
ROUND_BY = ((1, 6), (4, 7), (11, 8), (14, 9))


def pick(key, table):
    value = jnp.int32(0)
    for k, v in table:
        value = jnp.where(key == k, jnp.int32(v), value)
    return value


def split(x):
    high = x.astype(BF)
    return high, (x - high.astype(F32)).astype(BF)


def body(
    n_energy, side, lesser, greater, dft_hbm, tw_hbm, out,
    g_in, stage, turned, mirror_out, l_buf, g_buf, p_buf, held, dft, tw, y_hi, y_lo, spec, v_hi, v_lo, back,
    in_sem, own_sem, l_send, g_send, p_send, l_recv, g_recv, p_recv, r_recv, f_send,
):
    e = lax.axis_index("energy")
    t = lax.axis_index("tile")
    t2 = (t % side) * side + t // side
    off_diagonal = t2 != t
    local = g_in.shape[1]
    energies = n_energy * local
    half = energies // 2

    load_g = pltpu.make_async_copy(greater, g_in, in_sem.at[0])
    load_g.start()
    load_dft = pltpu.make_async_copy(dft_hbm, dft, in_sem.at[1])
    load_tw = pltpu.make_async_copy(tw_hbm, tw, in_sem.at[2])

    mirror = lambda k: (k % side) * side + k // side
    n_tile = side * side
    group = n_energy // 2
    base = (e // group) * group
    other = (e + group) % n_energy
    across = (t + n_tile // 2) % n_tile
    kind = pick(t, KINDS)
    relay = jnp.where(kind == ROUND, pick(t, ROUND_BY), across)
    round_from = pick(t, [(b, a) for a, b in ROUND_BY])
    source = jnp.where(round_from > 0, round_from, across)
    hands = pick(source, KINDS)
    hands = jnp.where(jnp.logical_and(hands == ROUND, round_from == 0), 0, hands)
    final = mirror(source)
    gets = pick(t2, KINDS)
    last = jnp.where(gets == ROUND, pick(t2, ROUND_BY), (t2 + n_tile // 2) % n_tile)

    def by_relay(how, frm, to):
        same = to // group == frm // group
        return jnp.logical_or(
            jnp.logical_and(how == HALF, same), jnp.logical_and(how == ROUND, (to + frm) % 4 == 0)
        )

    fourth = lambda m: 4 * m + (n_energy - e) % 4

    barrier = pltpu.get_barrier_semaphore()

    def greet(to, tile):
        pl.semaphore_signal(barrier, inc=1, device_id=(to, tile), device_id_type=MESH)

    @pl.loop(1, n_energy)
    def _(m):
        greet((e + m) % n_energy, t)

    @pl.when(off_diagonal)
    def _():
        @pl.loop(0, n_energy)
        def _(m):
            greet((e + m) % n_energy, t2)

    def greet_relay(how, tile):
        @pl.when(how > 0)
        def _():
            greet(e, tile)

    def greet_group(how, tile):
        @pl.when(how == HALF)
        def _():
            @pl.loop(0, group)
            def _(m):
                greet(base + m, tile)

        @pl.when(how == ROUND)
        def _():
            @pl.loop(0, n_energy // 4)
            def _(m):
                greet(fourth(m), tile)

    greet_relay(kind, relay)
    greet_relay(hands, source)
    greet_group(hands, final)
    greet_group(gets, last)

    def l_copy(h, to, frm):
        return pltpu.make_async_remote_copy(
            src_ref=lesser.at[:, :, h * n_energy + to],
            dst_ref=l_buf.at[h, :, pl.ds(pl.multiple_of(frm * local, local), local)],
            send_sem=l_send.at[h, to],
            recv_sem=l_recv.at[h, frm],
            device_id=(to, t),
            device_id_type=MESH,
        )

    def g_copy(h, to, frm):
        return pltpu.make_async_remote_copy(
            src_ref=mirror_out.at[:, :, h * n_energy + to],
            dst_ref=g_buf.at[h, :, pl.ds(pl.multiple_of(frm * local, local), local)],
            send_sem=g_send.at[h, to],
            recv_sem=g_recv.at[h, frm],
            device_id=(to, t2),
            device_id_type=MESH,
        )

    def first_leg(h, to):
        return pltpu.make_async_remote_copy(
            src_ref=mirror_out.at[:, :, h * n_energy + to],
            dst_ref=held.at[h, jnp.where(to // group == e // group, 0, 1), to % group],
            send_sem=g_send.at[h, to],
            recv_sem=r_recv.at[h, jnp.where(to // group == e // group, 0, 1), to % group],
            device_id=(jnp.where(kind == ROUND, e, (to // group) * group + e % group), relay),
            device_id_type=MESH,
        )

    def second_leg(h, k, m):
        frm = e if k == 0 else jnp.where(hands == ROUND, e, other)
        to = base + m if k == 0 else jnp.where(hands == ROUND, (base + group) % n_energy, base) + m
        return pltpu.make_async_remote_copy(
            src_ref=held.at[h, k, m],
            dst_ref=g_buf.at[h, :, pl.ds(pl.multiple_of(frm * local, local), local)],
            send_sem=f_send.at[h, k, m],
            recv_sem=g_recv.at[h, frm],
            device_id=(to, final),
            device_id_type=MESH,
        )

    def handed(k, m):
        quarter = jnp.logical_and(hands == ROUND, (m + e) % 4 == 0)
        return jnp.logical_or(hands == HALF, quarter) if k == 0 else quarter

    def p_copy(h, to, frm):
        return pltpu.make_async_remote_copy(
            src_ref=p_buf.at[h, :, pl.ds(pl.multiple_of(to * local, local), local)],
            dst_ref=out.at[:, :, h * n_energy + frm],
            send_sem=p_send.at[h, to],
            recv_sem=p_recv.at[h, frm],
            device_id=(to, t),
            device_id_type=MESH,
        )

    def l_own(h):
        return pltpu.make_async_copy(
            lesser.at[:, :, h * n_energy + e], l_buf.at[h, :, pl.ds(pl.multiple_of(e * local, local), local)], l_recv.at[h, e]
        )

    def g_own(h):
        return pltpu.make_async_copy(
            mirror_out.at[:, :, h * n_energy + e], g_buf.at[h, :, pl.ds(pl.multiple_of(e * local, local), local)], g_recv.at[h, e]
        )

    def p_own(h):
        return pltpu.make_async_copy(
            p_buf.at[h, :, pl.ds(pl.multiple_of(e * local, local), local)], out.at[:, :, h * n_energy + e], p_recv.at[h, e]
        )

    def send_l(h):
        @pl.loop(1, n_energy)
        def _(m):
            l_copy(h, (e + m) % n_energy, e).start()

        l_own(h).start()

    def send_legs(h):
        @pl.when(kind == ROUND)
        def _():
            @pl.loop(0, n_energy // 4)
            def _(m):
                first_leg(h, fourth(m)).start()

        @pl.when(kind == HALF)
        def _():
            @pl.loop(0, group)
            def _(m):
                first_leg(h, base + (e + m) % group).start()

    def send_g(h):
        @pl.loop(0, group)
        def _(m):
            for start in (base, (base + group) % n_energy):
                to = start + (e + m) % group
                own = jnp.logical_and(to == e, jnp.logical_not(off_diagonal))

                @pl.when(jnp.logical_not(jnp.logical_or(by_relay(kind, e, to), own)))
                def _():
                    g_copy(h, to, e).start()

        @pl.when(jnp.logical_not(off_diagonal))
        def _():
            g_own(h).start()

    def hand_on(h):
        @pl.loop(0, group)
        def _(step):
            m = (e + step) % group
            for k in range(2):

                @pl.when(handed(k, m))
                def _():
                    pltpu.make_async_copy(mirror_out.at[:, :, 0], held.at[h, k, m], r_recv.at[h, k, m]).wait()
                    second_leg(h, k, m).start()

    load_dft.start()
    load_tw.start()
    load_g.wait()

    low_lanes = lax.broadcasted_iota(jnp.int32, (32, 128), 1) < 64

    groups = stage.shape[0]

    @pl.loop(0, 2 * local // (4 * groups))
    def _(step):
        for k in range(groups):
            item = step * groups + k
            p = item // (local // 4)
            e0 = (item % (local // 4)) * 4
            for q in range(2):
                one = g_in[p, e0 + 2 * q]
                two = g_in[p, e0 + 2 * q + 1]
                stage[k, pl.ds(64 * q, 32, stride=2), :] = jnp.where(low_lanes, one, pltpu.roll(two, 64, 1))
                stage[k, pl.ds(64 * q + 1, 32, stride=2), :] = jnp.where(low_lanes, pltpu.roll(one, 64, 1), two)
        for k in range(groups):
            turned[k] = stage[k].T
        for k in range(groups):
            item = step * groups + k
            p = item // (local // 4)
            e0 = (item % (local // 4)) * 4
            for w in range(2):
                even = turned[k, pl.ds(64 * w, 32, stride=2), :]
                odd = turned[k, pl.ds(64 * w + 1, 32, stride=2), :]
                mirror_out[p, e0 + w] = jnp.where(low_lanes, even, pltpu.roll(odd, 64, 1))
                mirror_out[p, e0 + 2 + w] = jnp.where(low_lanes, pltpu.roll(even, 64, 1), odd)

    factor = 1.0 / (2 * energies * math.sqrt(energies))

    def put(column, re, im):
        hi, lo = split(re)
        y_hi[:half, column : column + 128] = hi
        y_lo[:half, column : column + 128] = lo
        hi, lo = split(im)
        y_hi[half:, column : column + 128] = hi
        y_lo[half:, column : column + 128] = lo

    def front(buf, h, base, sign):
        re0, re1 = buf[h, 0, :half], buf[h, 0, half:]
        im0, im1 = sign * buf[h, 1, :half], sign * buf[h, 1, half:]
        put(base, re0 + re1, im0 + im1)
        for q, re, im in (
            (1, re0 + im1, im0 - re1),
            (2, re0 - re1, im0 - im1),
            (3, re0 - im1, im0 + re1),
        ):
            c, s = tw[q - 1, 0], tw[q - 1, 1]
            put(base + 128 * q, re * c - im * s, re * s + im * c)

    def dots(rows, hi, lo, columns):
        dot = functools.partial(jnp.dot, preferred_element_type=F32)
        high, low = dft[0, rows], dft[1, rows]
        return dot(high, hi[:, columns]) + dot(high, lo[:, columns]) + dot(low, hi[:, columns])

    def wait_l(h):
        @pl.loop(1, n_energy)
        def _(m):
            l_copy(h, e, (e + n_energy - m) % n_energy).wait_recv()

        l_own(h).wait()

    def wait_g(h):
        @pl.loop(0, n_energy)
        def _(m):
            frm = (e + n_energy - m) % n_energy
            pltpu.make_async_copy(
                mirror_out.at[:, :, 0], g_buf.at[h, :, pl.ds(pl.multiple_of(frm * local, local), local)], g_recv.at[h, frm]
            ).wait()

    def compute_l(h):
        front(l_buf, h, 0, 1.0)
        for c in range(2):
            columns = slice(256 * c, 256 * c + 256)
            spec[:, columns] = dots(slice(None), y_hi, y_lo, columns)

    def compute_g(h):
        front(g_buf, h, 512, -1.0)
        for c in range(2, 4):
            columns = slice(256 * c, 256 * c + 256)
            spec[:, columns] = dots(slice(None), y_hi, y_lo, columns)
        for c in range(4):
            one, two = slice(128 * c, 128 * c + 128), slice(512 + 128 * c, 640 + 128 * c)
            ar, ai = spec[:half, one], spec[half:, one]
            br, bi = spec[:half, two], spec[half:, two]
            hi, lo = split(ar * br + ai * bi)
            v_hi[:half, one] = hi
            v_lo[:half, one] = lo
            hi, lo = split(ar * bi - ai * br)
            v_hi[half:, one] = hi
            v_lo[half:, one] = lo

    def finish(h, part):
        blocks = [slice(local * (2 * k + part), local * (2 * k + part) + local) for k in range(n_energy // 4)]
        later = [slice(half + b.start, half + b.stop) for b in blocks]
        take = lambda ref, index, rows: jnp.concatenate([ref[(*index, r)] for r in rows])
        count = half // 2
        for c in range(2):
            columns = slice(256 * c, 256 * c + 256)
            for rows, to in ((blocks, slice(0, count)), (later, slice(count, half))):
                dot = functools.partial(jnp.dot, preferred_element_type=F32)
                high, low = take(dft, (0,), rows), take(dft, (1,), rows)
                back[to, columns] = (
                    dot(high, v_hi[:, columns]) + dot(high, v_lo[:, columns]) + dot(low, v_hi[:, columns])
                )
        terms = [(back[:count, :128], back[count:half, :128])]
        for q in (1, 2, 3):
            re, im = back[:count, 128 * q : 128 * q + 128], back[count:half, 128 * q : 128 * q + 128]
            c, s = take(tw, (q - 1, 0), blocks), take(tw, (q - 1, 1), blocks)
            terms.append((re * c - im * s, re * s + im * c))
        (r0, i0), (r1, i1), (r2, i2), (r3, i3) = terms
        values = (
            (0, blocks, i0 + i1 + i2 + i3),
            (1, blocks, r0 + r1 + r2 + r3),
            (0, later, i0 - r1 - i2 + r3),
            (1, later, r0 + i1 - r2 - i3),
        )
        for p, rows, value in values:
            for k, r in enumerate(rows):
                p_buf[h, p, r] = value[local * k : local * k + local] * -factor

    def send_p(h, part):
        @pl.loop(0, group)
        def _(m):
            to = 2 * ((e // 2 + m) % group) + part

            @pl.when(to != e)
            def _():
                p_copy(h, to, e).start()

            @pl.when(to == e)
            def _():
                p_own(h).start()

    def drain_l(h):
        @pl.loop(1, n_energy)
        def _(m):
            l_copy(h, (e + m) % n_energy, e).wait_send()

    def drain_g(h):
        @pl.loop(1, n_energy)
        def _(m):
            g_copy(h, (e + m) % n_energy, e).wait_send()

        @pl.when(off_diagonal)
        def _():
            g_copy(h, e, e).wait_send()

        @pl.loop(0, group)
        def _(m):
            for k in range(2):

                @pl.when(handed(k, m))
                def _():
                    second_leg(h, k, m).wait_send()

    def drain_p(h):
        @pl.loop(1, n_energy)
        def _(m):
            to = (e + m) % n_energy
            p_copy(h, to, e).wait_send()
            p_copy(h, e, to).wait_recv()

        p_own(h).wait()

    signals = n_energy - 1 + jnp.where(off_diagonal, n_energy, 0)
    for how in (kind, hands):
        signals += jnp.where(how > 0, 1, 0)
    for how in (hands, gets):
        signals += jnp.where(how == HALF, group, 0) + jnp.where(how == ROUND, n_energy // 4, 0)
    pl.semaphore_wait(barrier, signals)

    for h in range(2):
        send_legs(h)
        send_g(h)
        send_l(h)
        hand_on(h)
    load_dft.wait()
    load_tw.wait()

    @pl.loop(0, 2)
    def _(h):
        wait_l(h)
        compute_l(h)
        wait_g(h)
        compute_g(h)
        for part in range(2):
            finish(h, part)
            send_p(h, part)

    @pl.loop(0, 2)
    def _(h):
        drain_l(h)
        drain_g(h)
        drain_p(h)


def on_device(lesser, greater):
    n_energy = lax.axis_size("energy")
    side = math.isqrt(lax.axis_size("tile"))
    local, cells = lesser.shape[1], lesser.shape[3]
    rows = cells // 128
    energies = n_energy * local
    dft, twiddle = tables(energies, 128)
    any_space = pl.BlockSpec(memory_space=pltpu.HBM)
    half = energies // 2
    out = pl.pallas_call(
        functools.partial(body, n_energy, side),
        out_shape=jax.ShapeDtypeStruct((2, local, rows, 128), F32),
        in_specs=[any_space] * 4,
        out_specs=any_space,
        scratch_shapes=[
            pltpu.VMEM((2, local, rows, 128), F32),
            pltpu.VMEM((4, 128, 128), F32),
            pltpu.VMEM((4, 128, 128), F32),
            pltpu.VMEM((2, local, rows, 128), F32),
            pltpu.VMEM((2, 2, energies, 128), F32),
            pltpu.VMEM((2, 2, energies, 128), F32),
            pltpu.VMEM((2, 2, energies, 128), F32),
            pltpu.VMEM((2, 2, n_energy // 2, 2, local, 128), F32),
            pltpu.VMEM((2, energies, energies), BF),
            pltpu.VMEM((3, 2, half, 128), F32),
            pltpu.VMEM((energies, 1024), BF),
            pltpu.VMEM((energies, 1024), BF),
            pltpu.VMEM((energies, 1024), F32),
            pltpu.VMEM((energies, 512), BF),
            pltpu.VMEM((energies, 512), BF),
            pltpu.VMEM((energies, 512), F32),
            pltpu.SemaphoreType.DMA((3,)),
            pltpu.SemaphoreType.DMA((2,)),
        ]
        + [pltpu.SemaphoreType.DMA((2, n_energy))] * 6
        + [pltpu.SemaphoreType.DMA((2, 2, n_energy // 2))] * 2,
        compiler_params=pltpu.CompilerParams(
            collective_id=0, has_side_effects=True, vmem_limit_bytes=40 * 2**20
        ),
        name="correlate",
    )(
        pltpu.with_memory_space_constraint(lesser.reshape(2, local, rows, 128), pltpu.HBM),
        pltpu.with_memory_space_constraint(greater.reshape(2, local, rows, 128), pltpu.HBM),
        pltpu.with_memory_space_constraint(jnp.asarray(dft), pltpu.HBM),
        pltpu.with_memory_space_constraint(jnp.asarray(twiddle), pltpu.HBM),
    )
    return out.reshape(2, local, 1, cells)


def solution(mesh):
    return jax.shard_map(
        on_device,
        mesh=mesh,
        in_specs=(P(None, "energy", "tile", None), P(None, "energy", "tile", None)),
        out_specs=P(None, "energy", "tile", None),
        check_vma=False,
    )
```

```python
import functools
import math

import jax
import jax.numpy as jnp
import ml_dtypes
import numpy as np
from jax import lax
from jax.experimental import pallas as pl
from jax.experimental.pallas import tpu as pltpu
from jax.sharding import PartitionSpec as P

MESH = pl.DeviceIdType.MESH
BF = jnp.bfloat16
F32 = jnp.float32


def tables(energies, lanes):
    length = 2 * energies
    quarter = length // 4
    n = np.arange(quarter)
    angle = 2.0 * np.pi * (np.outer(n, n) % quarter) / quarter
    cos, sin = np.cos(angle), np.sin(angle)
    full = np.block([[cos, sin], [-sin, cos]]).astype(np.float32)
    high = full.astype(ml_dtypes.bfloat16)
    low = (full - high.astype(np.float32)).astype(ml_dtypes.bfloat16)
    rows = []
    for q in (1, 2, 3):
        turn = 2.0 * np.pi * ((n * q) % length) / length
        rows.append(np.stack([np.cos(turn), -np.sin(turn)]))
    twiddle = np.stack(rows).astype(np.float32)
    twiddle = np.ascontiguousarray(np.broadcast_to(twiddle[..., None], twiddle.shape + (lanes,)))
    return np.stack([high, low]), twiddle


HALF, ROUND = 1, 2
KINDS = tuple((k, HALF) for k in (2, 3, 6, 7, 8, 9, 12, 13)) + tuple((k, ROUND) for k in (1, 4, 11, 14))
ROUND_BY = ((1, 7), (4, 6), (11, 9), (14, 8))


def pick(key, table):
    value = jnp.int32(0)
    for k, v in table:
        value = jnp.where(key == k, jnp.int32(v), value)
    return value


def split(x):
    high = x.astype(BF)
    return high, (x - high.astype(F32)).astype(BF)


def body(
    n_energy, side, lesser, greater, dft_hbm, tw_hbm, out,
    g_in, stage, turned, mirror_out, l_buf, g_buf, p_buf, held, dft, tw, y_hi, y_lo, spec, v_hi, v_lo, back,
    in_sem, own_sem, l_send, g_send, p_send, l_recv, g_recv, p_recv, r_recv, f_send,
):
    e = lax.axis_index("energy")
    t = lax.axis_index("tile")
    t2 = (t % side) * side + t // side
    off_diagonal = t2 != t
    local = g_in.shape[1]
    energies = n_energy * local
    half = energies // 2

    load_g = pltpu.make_async_copy(greater, g_in, in_sem.at[0])
    load_g.start()
    load_dft = pltpu.make_async_copy(dft_hbm, dft, in_sem.at[1])
    load_tw = pltpu.make_async_copy(tw_hbm, tw, in_sem.at[2])

    mirror = lambda k: (k % side) * side + k // side
    n_tile = side * side
    group = n_energy // 2
    base = (e // group) * group
    other = (e + group) % n_energy
    across = (t + n_tile // 2) % n_tile
    kind = pick(t, KINDS)
    relay = jnp.where(kind == ROUND, pick(t, ROUND_BY), across)
    round_from = pick(t, [(b, a) for a, b in ROUND_BY])
    source = jnp.where(round_from > 0, round_from, across)
    hands = pick(source, KINDS)
    hands = jnp.where(jnp.logical_and(hands == ROUND, round_from == 0), 0, hands)
    final = mirror(source)
    gets = pick(t2, KINDS)
    last = jnp.where(gets == ROUND, pick(t2, ROUND_BY), (t2 + n_tile // 2) % n_tile)

    def by_relay(how, frm, to):
        same = to // group == frm // group
        return jnp.logical_or(
            jnp.logical_and(how == HALF, same), jnp.logical_and(how == ROUND, (to + frm) % 4 == 0)
        )

    fourth = lambda m: 4 * m + (n_energy - e) % 4

    barrier = pltpu.get_barrier_semaphore()

    def greet(to, tile):
        pl.semaphore_signal(barrier, inc=1, device_id=(to, tile), device_id_type=MESH)

    @pl.loop(1, n_energy)
    def _(m):
        greet((e + m) % n_energy, t)

    @pl.when(off_diagonal)
    def _():
        @pl.loop(0, n_energy)
        def _(m):
            to = (e + m) % n_energy

            @pl.when(jnp.logical_not(by_relay(kind, e, to)))
            def _():
                greet(to, t2)

    def greet_relay(how, tile):
        @pl.when(how > 0)
        def _():
            greet(e, tile)

    def greet_group(how, tile):
        @pl.when(how == HALF)
        def _():
            @pl.loop(0, group)
            def _(m):
                greet(base + m, tile)

        @pl.when(how == ROUND)
        def _():
            @pl.loop(0, n_energy // 4)
            def _(m):
                greet(fourth(m), tile)

    greet_relay(kind, relay)
    greet_relay(hands, source)
    greet_group(hands, final)
    greet_group(gets, last)

    def l_copy(h, to, frm):
        return pltpu.make_async_remote_copy(
            src_ref=lesser.at[:, :, h * n_energy + to],
            dst_ref=l_buf.at[h, :, pl.ds(pl.multiple_of(frm * local, local), local)],
            send_sem=l_send.at[h, to],
            recv_sem=l_recv.at[h, frm],
            device_id=(to, t),
            device_id_type=MESH,
        )

    def g_copy(h, to, frm):
        return pltpu.make_async_remote_copy(
            src_ref=mirror_out.at[:, :, h * n_energy + to],
            dst_ref=g_buf.at[h, :, pl.ds(pl.multiple_of(frm * local, local), local)],
            send_sem=g_send.at[h, to],
            recv_sem=g_recv.at[h, frm],
            device_id=(to, t2),
            device_id_type=MESH,
        )

    def first_leg(h, to):
        return pltpu.make_async_remote_copy(
            src_ref=mirror_out.at[:, :, h * n_energy + to],
            dst_ref=held.at[h, jnp.where(to // group == e // group, 0, 1), to % group],
            send_sem=g_send.at[h, to],
            recv_sem=r_recv.at[h, jnp.where(to // group == e // group, 0, 1), to % group],
            device_id=(jnp.where(kind == ROUND, e, (to // group) * group + e % group), relay),
            device_id_type=MESH,
        )

    def second_leg(h, k, m):
        frm = e if k == 0 else jnp.where(hands == ROUND, e, other)
        to = base + m if k == 0 else jnp.where(hands == ROUND, (base + group) % n_energy, base) + m
        return pltpu.make_async_remote_copy(
            src_ref=held.at[h, k, m],
            dst_ref=g_buf.at[h, :, pl.ds(pl.multiple_of(frm * local, local), local)],
            send_sem=f_send.at[h, k, m],
            recv_sem=g_recv.at[h, frm],
            device_id=(to, final),
            device_id_type=MESH,
        )

    def handed(k, m):
        quarter = jnp.logical_and(hands == ROUND, (m + e) % 4 == 0)
        return jnp.logical_or(hands == HALF, quarter) if k == 0 else quarter

    def p_copy(h, to, frm):
        return pltpu.make_async_remote_copy(
            src_ref=p_buf.at[h, :, pl.ds(pl.multiple_of(to * local, local), local)],
            dst_ref=out.at[:, :, h * n_energy + frm],
            send_sem=p_send.at[h, to],
            recv_sem=p_recv.at[h, frm],
            device_id=(to, t),
            device_id_type=MESH,
        )

    def l_own(h):
        return pltpu.make_async_copy(
            lesser.at[:, :, h * n_energy + e], l_buf.at[h, :, pl.ds(pl.multiple_of(e * local, local), local)], l_recv.at[h, e]
        )

    def g_own(h):
        return pltpu.make_async_copy(
            mirror_out.at[:, :, h * n_energy + e], g_buf.at[h, :, pl.ds(pl.multiple_of(e * local, local), local)], g_recv.at[h, e]
        )

    def p_own(h):
        return pltpu.make_async_copy(
            p_buf.at[h, :, pl.ds(pl.multiple_of(e * local, local), local)], out.at[:, :, h * n_energy + e], p_recv.at[h, e]
        )

    def send_l(h):
        @pl.loop(1, n_energy)
        def _(m):
            l_copy(h, (e + m) % n_energy, e).start()

        l_own(h).start()

    def send_legs(h):
        @pl.when(kind == ROUND)
        def _():
            @pl.loop(0, n_energy // 4)
            def _(m):
                first_leg(h, fourth(m)).start()

        @pl.when(kind == HALF)
        def _():
            @pl.loop(0, group)
            def _(m):
                first_leg(h, base + (e + m) % group).start()

    def send_g(h):
        @pl.loop(0, group)
        def _(m):
            for start in (base, (base + group) % n_energy):
                to = start + (e + m) % group
                own = jnp.logical_and(to == e, jnp.logical_not(off_diagonal))

                @pl.when(jnp.logical_not(jnp.logical_or(by_relay(kind, e, to), own)))
                def _():
                    g_copy(h, to, e).start()

        @pl.when(jnp.logical_not(off_diagonal))
        def _():
            g_own(h).start()

    def hand_on(h):
        @pl.loop(0, group)
        def _(step):
            m = (e + step) % group
            for k in range(2):

                @pl.when(handed(k, m))
                def _():
                    pltpu.make_async_copy(mirror_out.at[:, :, 0], held.at[h, k, m], r_recv.at[h, k, m]).wait()
                    second_leg(h, k, m).start()

    load_dft.start()
    load_tw.start()
    load_g.wait()

    low_lanes = lax.broadcasted_iota(jnp.int32, (32, 128), 1) < 64

    groups = stage.shape[0]

    @pl.loop(0, 2 * local // (4 * groups))
    def _(step):
        for k in range(groups):
            item = step * groups + k
            p = item // (local // 4)
            e0 = (item % (local // 4)) * 4
            for q in range(2):
                one = g_in[p, e0 + 2 * q]
                two = g_in[p, e0 + 2 * q + 1]
                stage[k, pl.ds(64 * q, 32, stride=2), :] = jnp.where(low_lanes, one, pltpu.roll(two, 64, 1))
                stage[k, pl.ds(64 * q + 1, 32, stride=2), :] = jnp.where(low_lanes, pltpu.roll(one, 64, 1), two)
        for k in range(groups):
            turned[k] = stage[k].T
        for k in range(groups):
            item = step * groups + k
            p = item // (local // 4)
            e0 = (item % (local // 4)) * 4
            for w in range(2):
                even = turned[k, pl.ds(64 * w, 32, stride=2), :]
                odd = turned[k, pl.ds(64 * w + 1, 32, stride=2), :]
                mirror_out[p, e0 + w] = jnp.where(low_lanes, even, pltpu.roll(odd, 64, 1))
                mirror_out[p, e0 + 2 + w] = jnp.where(low_lanes, pltpu.roll(even, 64, 1), odd)

    factor = 1.0 / (2 * energies * math.sqrt(energies))

    def put(column, re, im):
        hi, lo = split(re)
        y_hi[:half, column : column + 128] = hi
        y_lo[:half, column : column + 128] = lo
        hi, lo = split(im)
        y_hi[half:, column : column + 128] = hi
        y_lo[half:, column : column + 128] = lo

    def front(buf, h, base, sign):
        re0, re1 = buf[h, 0, :half], buf[h, 0, half:]
        im0, im1 = sign * buf[h, 1, :half], sign * buf[h, 1, half:]
        put(base, re0 + re1, im0 + im1)
        for q, re, im in (
            (1, re0 + im1, im0 - re1),
            (2, re0 - re1, im0 - im1),
            (3, re0 - im1, im0 + re1),
        ):
            c, s = tw[q - 1, 0], tw[q - 1, 1]
            put(base + 128 * q, re * c - im * s, re * s + im * c)

    def dots(rows, hi, lo, columns):
        dot = functools.partial(jnp.dot, preferred_element_type=F32)
        high, low = dft[0, rows], dft[1, rows]
        return dot(high, hi[:, columns]) + dot(high, lo[:, columns]) + dot(low, hi[:, columns])

    def wait_l(h):
        @pl.loop(1, n_energy)
        def _(m):
            l_copy(h, e, (e + n_energy - m) % n_energy).wait_recv()

        l_own(h).wait()

    def wait_g(h):
        @pl.loop(0, n_energy)
        def _(m):
            frm = (e + n_energy - m) % n_energy
            pltpu.make_async_copy(
                mirror_out.at[:, :, 0], g_buf.at[h, :, pl.ds(pl.multiple_of(frm * local, local), local)], g_recv.at[h, frm]
            ).wait()

    def compute_l(h):
        front(l_buf, h, 0, 1.0)
        for c in range(2):
            columns = slice(256 * c, 256 * c + 256)
            spec[:, columns] = dots(slice(None), y_hi, y_lo, columns)

    def compute_g(h):
        front(g_buf, h, 512, -1.0)
        for c in range(2, 4):
            columns = slice(256 * c, 256 * c + 256)
            spec[:, columns] = dots(slice(None), y_hi, y_lo, columns)
        for c in range(4):
            one, two = slice(128 * c, 128 * c + 128), slice(512 + 128 * c, 640 + 128 * c)
            ar, ai = spec[:half, one], spec[half:, one]
            br, bi = spec[:half, two], spec[half:, two]
            hi, lo = split(ar * br + ai * bi)
            v_hi[:half, one] = hi
            v_lo[:half, one] = lo
            hi, lo = split(ar * bi - ai * br)
            v_hi[half:, one] = hi
            v_lo[half:, one] = lo

    def finish(h, part):
        blocks = [slice(local * (2 * k + part), local * (2 * k + part) + local) for k in range(n_energy // 4)]
        later = [slice(half + b.start, half + b.stop) for b in blocks]
        take = lambda ref, index, rows: jnp.concatenate([ref[(*index, r)] for r in rows])
        count = half // 2
        for c in range(2):
            columns = slice(256 * c, 256 * c + 256)
            for rows, to in ((blocks, slice(0, count)), (later, slice(count, half))):
                dot = functools.partial(jnp.dot, preferred_element_type=F32)
                high, low = take(dft, (0,), rows), take(dft, (1,), rows)
                back[to, columns] = (
                    dot(high, v_hi[:, columns]) + dot(high, v_lo[:, columns]) + dot(low, v_hi[:, columns])
                )
        terms = [(back[:count, :128], back[count:half, :128])]
        for q in (1, 2, 3):
            re, im = back[:count, 128 * q : 128 * q + 128], back[count:half, 128 * q : 128 * q + 128]
            c, s = take(tw, (q - 1, 0), blocks), take(tw, (q - 1, 1), blocks)
            terms.append((re * c - im * s, re * s + im * c))
        (r0, i0), (r1, i1), (r2, i2), (r3, i3) = terms
        values = (
            (0, blocks, i0 + i1 + i2 + i3),
            (1, blocks, r0 + r1 + r2 + r3),
            (0, later, i0 - r1 - i2 + r3),
            (1, later, r0 + i1 - r2 - i3),
        )
        for p, rows, value in values:
            for k, r in enumerate(rows):
                p_buf[h, p, r] = value[local * k : local * k + local] * -factor

    def send_p(h, part):
        @pl.loop(0, group)
        def _(m):
            to = 2 * ((e // 2 + m) % group) + part

            @pl.when(to != e)
            def _():
                p_copy(h, to, e).start()

            @pl.when(to == e)
            def _():
                p_own(h).start()

    def drain_l(h):
        @pl.loop(1, n_energy)
        def _(m):
            l_copy(h, (e + m) % n_energy, e).wait_send()

    def drain_g(h):
        @pl.loop(1, n_energy)
        def _(m):
            g_copy(h, (e + m) % n_energy, e).wait_send()

        @pl.when(off_diagonal)
        def _():
            g_copy(h, e, e).wait_send()

        @pl.loop(0, group)
        def _(m):
            for k in range(2):

                @pl.when(handed(k, m))
                def _():
                    second_leg(h, k, m).wait_send()

    def drain_p(h):
        @pl.loop(1, n_energy)
        def _(m):
            to = (e + m) % n_energy
            p_copy(h, to, e).wait_send()
            p_copy(h, e, to).wait_recv()

        p_own(h).wait()

    signals = n_energy - 1 + jnp.where(off_diagonal, n_energy, 0)
    signals -= jnp.where(kind == HALF, group, 0) + jnp.where(kind == ROUND, n_energy // 4, 0)
    for how in (kind, hands):
        signals += jnp.where(how > 0, 1, 0)
    for how in (hands, gets):
        signals += jnp.where(how == HALF, group, 0) + jnp.where(how == ROUND, n_energy // 4, 0)
    pl.semaphore_wait(barrier, signals)

    for h in range(2):
        send_legs(h)
        send_g(h)
        send_l(h)
        hand_on(h)
    load_dft.wait()
    load_tw.wait()

    @pl.loop(0, 2)
    def _(h):
        wait_l(h)
        compute_l(h)
        wait_g(h)
        compute_g(h)
        for part in range(2):
            finish(h, part)
            send_p(h, part)

    @pl.loop(0, 2)
    def _(h):
        drain_l(h)
        drain_g(h)
        drain_p(h)


def on_device(lesser, greater):
    n_energy = lax.axis_size("energy")
    side = math.isqrt(lax.axis_size("tile"))
    local, cells = lesser.shape[1], lesser.shape[3]
    rows = cells // 128
    energies = n_energy * local
    dft, twiddle = tables(energies, 128)
    any_space = pl.BlockSpec(memory_space=pltpu.HBM)
    half = energies // 2
    out = pl.pallas_call(
        functools.partial(body, n_energy, side),
        out_shape=jax.ShapeDtypeStruct((2, local, rows, 128), F32),
        in_specs=[any_space] * 4,
        out_specs=any_space,
        scratch_shapes=[
            pltpu.VMEM((2, local, rows, 128), F32),
            pltpu.VMEM((4, 128, 128), F32),
            pltpu.VMEM((4, 128, 128), F32),
            pltpu.VMEM((2, local, rows, 128), F32),
            pltpu.VMEM((2, 2, energies, 128), F32),
            pltpu.VMEM((2, 2, energies, 128), F32),
            pltpu.VMEM((2, 2, energies, 128), F32),
            pltpu.VMEM((2, 2, n_energy // 2, 2, local, 128), F32),
            pltpu.VMEM((2, energies, energies), BF),
            pltpu.VMEM((3, 2, half, 128), F32),
            pltpu.VMEM((energies, 1024), BF),
            pltpu.VMEM((energies, 1024), BF),
            pltpu.VMEM((energies, 1024), F32),
            pltpu.VMEM((energies, 512), BF),
            pltpu.VMEM((energies, 512), BF),
            pltpu.VMEM((energies, 512), F32),
            pltpu.SemaphoreType.DMA((3,)),
            pltpu.SemaphoreType.DMA((2,)),
        ]
        + [pltpu.SemaphoreType.DMA((2, n_energy))] * 6
        + [pltpu.SemaphoreType.DMA((2, 2, n_energy // 2))] * 2,
        compiler_params=pltpu.CompilerParams(
            collective_id=0, has_side_effects=True, vmem_limit_bytes=40 * 2**20
        ),
        name="correlate",
    )(
        pltpu.with_memory_space_constraint(lesser.reshape(2, local, rows, 128), pltpu.HBM),
        pltpu.with_memory_space_constraint(greater.reshape(2, local, rows, 128), pltpu.HBM),
        pltpu.with_memory_space_constraint(jnp.asarray(dft), pltpu.HBM),
        pltpu.with_memory_space_constraint(jnp.asarray(twiddle), pltpu.HBM),
    )
    return out.reshape(2, local, 1, cells)


def solution(mesh):
    return jax.shard_map(
        on_device,
        mesh=mesh,
        in_specs=(P(None, "energy", "tile", None), P(None, "energy", "tile", None)),
        out_specs=P(None, "energy", "tile", None),
        check_vma=False,
    )
```

```python
import functools
import math

import jax
import jax.numpy as jnp
import ml_dtypes
import numpy as np
from jax import lax
from jax.experimental import pallas as pl
from jax.experimental.pallas import tpu as pltpu
from jax.sharding import PartitionSpec as P

MESH = pl.DeviceIdType.MESH
BF = jnp.bfloat16
F32 = jnp.float32


def tables(energies, lanes):
    length = 2 * energies
    quarter = length // 4
    n = np.arange(quarter)
    angle = 2.0 * np.pi * (np.outer(n, n) % quarter) / quarter
    cos, sin = np.cos(angle), np.sin(angle)
    full = np.block([[cos, sin], [-sin, cos]]).astype(np.float32)
    high = full.astype(ml_dtypes.bfloat16)
    low = (full - high.astype(np.float32)).astype(ml_dtypes.bfloat16)
    rows = []
    for q in (1, 2, 3):
        turn = 2.0 * np.pi * ((n * q) % length) / length
        rows.append(np.stack([np.cos(turn), -np.sin(turn)]))
    twiddle = np.stack(rows).astype(np.float32)
    twiddle = np.ascontiguousarray(np.broadcast_to(twiddle[..., None], twiddle.shape + (lanes,)))
    return np.stack([high, low]), twiddle


HALF, ROUND = 1, 2
KINDS = tuple((k, HALF) for k in (2, 3, 6, 7, 8, 9, 12, 13)) + tuple((k, ROUND) for k in (1, 4, 11, 14))
ROUND_BY = ((1, 7), (4, 6), (11, 9), (14, 8))


def pick(key, table):
    value = jnp.int32(0)
    for k, v in table:
        value = jnp.where(key == k, jnp.int32(v), value)
    return value


def split(x):
    high = x.astype(BF)
    return high, (x - high.astype(F32)).astype(BF)


def body(
    n_energy, side, lesser, greater, dft_hbm, tw_hbm, out,
    g_in, stage, turned, mirror_out, l_buf, g_buf, p_buf, held, dft, tw, y_hi, y_lo, spec, v_hi, v_lo, back,
    in_sem, own_sem, l_send, g_send, p_send, l_recv, g_recv, p_recv, r_recv, f_send,
):
    e = lax.axis_index("energy")
    t = lax.axis_index("tile")
    t2 = (t % side) * side + t // side
    off_diagonal = t2 != t
    local = g_in.shape[1]
    energies = n_energy * local
    half = energies // 2

    load_g = pltpu.make_async_copy(greater, g_in, in_sem.at[0])
    load_g.start()
    load_dft = pltpu.make_async_copy(dft_hbm, dft, in_sem.at[1])
    load_tw = pltpu.make_async_copy(tw_hbm, tw, in_sem.at[2])

    mirror = lambda k: (k % side) * side + k // side
    n_tile = side * side
    group = n_energy // 2
    base = (e // group) * group
    other = (e + group) % n_energy
    across = (t + n_tile // 2) % n_tile
    kind = pick(t, KINDS)
    relay = jnp.where(kind == ROUND, pick(t, ROUND_BY), across)
    round_from = pick(t, [(b, a) for a, b in ROUND_BY])
    source = jnp.where(round_from > 0, round_from, across)
    hands = pick(source, KINDS)
    hands = jnp.where(jnp.logical_and(hands == ROUND, round_from == 0), 0, hands)
    final = mirror(source)
    gets = pick(t2, KINDS)
    last = jnp.where(gets == ROUND, pick(t2, ROUND_BY), (t2 + n_tile // 2) % n_tile)

    def by_relay(how, frm, to):
        same = to // group == frm // group
        return jnp.logical_or(
            jnp.logical_and(how == HALF, same), jnp.logical_and(how == ROUND, (to + frm) % 4 == 0)
        )

    fourth = lambda m: 4 * m + (n_energy - e) % 4

    barrier = pltpu.get_barrier_semaphore()

    def greet(to, tile):
        pl.semaphore_signal(barrier, inc=1, device_id=(to, tile), device_id_type=MESH)

    @pl.loop(1, n_energy)
    def _(m):
        greet((e + m) % n_energy, t)

    @pl.when(off_diagonal)
    def _():
        @pl.loop(0, n_energy)
        def _(m):
            to = (e + m) % n_energy

            @pl.when(jnp.logical_not(by_relay(kind, e, to)))
            def _():
                greet(to, t2)

    def greet_relay(how, tile):
        @pl.when(how > 0)
        def _():
            greet(e, tile)

    def greet_group(how, tile):
        @pl.when(how == HALF)
        def _():
            @pl.loop(0, group)
            def _(m):
                greet(base + m, tile)

        @pl.when(how == ROUND)
        def _():
            @pl.loop(0, n_energy // 4)
            def _(m):
                greet(fourth(m), tile)

    greet_relay(kind, relay)
    greet_relay(hands, source)
    greet_group(hands, final)
    greet_group(gets, last)

    def l_copy(h, to, frm):
        return pltpu.make_async_remote_copy(
            src_ref=lesser.at[:, :, h * n_energy + to],
            dst_ref=l_buf.at[h, :, pl.ds(pl.multiple_of(frm * local, local), local)],
            send_sem=l_send.at[h, to],
            recv_sem=l_recv.at[h, frm],
            device_id=(to, t),
            device_id_type=MESH,
        )

    def g_copy(h, to, frm):
        return pltpu.make_async_remote_copy(
            src_ref=mirror_out.at[:, :, h * n_energy + to],
            dst_ref=g_buf.at[h, :, pl.ds(pl.multiple_of(frm * local, local), local)],
            send_sem=g_send.at[h, to],
            recv_sem=g_recv.at[h, frm],
            device_id=(to, t2),
            device_id_type=MESH,
        )

    def first_leg(h, to):
        return pltpu.make_async_remote_copy(
            src_ref=mirror_out.at[:, :, h * n_energy + to],
            dst_ref=held.at[h, jnp.where(to // group == e // group, 0, 1), to % group],
            send_sem=g_send.at[h, to],
            recv_sem=r_recv.at[h, jnp.where(to // group == e // group, 0, 1), to % group],
            device_id=(jnp.where(kind == ROUND, e, (to // group) * group + e % group), relay),
            device_id_type=MESH,
        )

    def second_leg(h, k, m):
        frm = e if k == 0 else jnp.where(hands == ROUND, e, other)
        to = base + m if k == 0 else jnp.where(hands == ROUND, (base + group) % n_energy, base) + m
        return pltpu.make_async_remote_copy(
            src_ref=held.at[h, k, m],
            dst_ref=g_buf.at[h, :, pl.ds(pl.multiple_of(frm * local, local), local)],
            send_sem=f_send.at[h, k, m],
            recv_sem=g_recv.at[h, frm],
            device_id=(to, final),
            device_id_type=MESH,
        )

    def handed(k, m):
        quarter = jnp.logical_and(hands == ROUND, (m + e) % 4 == 0)
        return jnp.logical_or(hands == HALF, quarter) if k == 0 else quarter

    def p_copy(h, to, frm):
        return pltpu.make_async_remote_copy(
            src_ref=p_buf.at[h, :, pl.ds(pl.multiple_of(to * local, local), local)],
            dst_ref=out.at[:, :, h * n_energy + frm],
            send_sem=p_send.at[h, to],
            recv_sem=p_recv.at[h, frm],
            device_id=(to, t),
            device_id_type=MESH,
        )

    def l_own(h):
        return pltpu.make_async_copy(
            lesser.at[:, :, h * n_energy + e], l_buf.at[h, :, pl.ds(pl.multiple_of(e * local, local), local)], l_recv.at[h, e]
        )

    def g_own(h):
        return pltpu.make_async_copy(
            mirror_out.at[:, :, h * n_energy + e], g_buf.at[h, :, pl.ds(pl.multiple_of(e * local, local), local)], g_recv.at[h, e]
        )

    def p_own(h):
        return pltpu.make_async_copy(
            p_buf.at[h, :, pl.ds(pl.multiple_of(e * local, local), local)], out.at[:, :, h * n_energy + e], p_recv.at[h, e]
        )

    def send_l(h):
        @pl.loop(1, n_energy)
        def _(m):
            l_copy(h, (e + m) % n_energy, e).start()

        l_own(h).start()

    def send_legs(h):
        @pl.when(kind == ROUND)
        def _():
            @pl.loop(0, n_energy // 4)
            def _(m):
                first_leg(h, fourth(m)).start()

        @pl.when(kind == HALF)
        def _():
            @pl.loop(0, group)
            def _(m):
                first_leg(h, base + (e + m) % group).start()

    def send_g(h):
        @pl.loop(0, group)
        def _(m):
            for start in (base, (base + group) % n_energy):
                to = start + (e + m) % group
                own = jnp.logical_and(to == e, jnp.logical_not(off_diagonal))

                @pl.when(jnp.logical_not(jnp.logical_or(by_relay(kind, e, to), own)))
                def _():
                    g_copy(h, to, e).start()

        @pl.when(jnp.logical_not(off_diagonal))
        def _():
            g_own(h).start()

    def hand_on(h):
        @pl.loop(0, group)
        def _(step):
            m = (e + step) % group
            for k in range(2):

                @pl.when(handed(k, m))
                def _():
                    pltpu.make_async_copy(mirror_out.at[:, :, 0], held.at[h, k, m], r_recv.at[h, k, m]).wait()
                    second_leg(h, k, m).start()

    load_dft.start()
    load_tw.start()
    load_g.wait()

    low_lanes = lax.broadcasted_iota(jnp.int32, (32, 128), 1) < 64

    groups = stage.shape[0]

    @pl.loop(0, 2 * local // (4 * groups))
    def _(step):
        for k in range(groups):
            item = step * groups + k
            p = item // (local // 4)
            e0 = (item % (local // 4)) * 4
            for q in range(2):
                one = g_in[p, e0 + 2 * q]
                two = g_in[p, e0 + 2 * q + 1]
                stage[k, pl.ds(64 * q, 32, stride=2), :] = jnp.where(low_lanes, one, pltpu.roll(two, 64, 1))
                stage[k, pl.ds(64 * q + 1, 32, stride=2), :] = jnp.where(low_lanes, pltpu.roll(one, 64, 1), two)
        for k in range(groups):
            turned[k] = stage[k].T
        for k in range(groups):
            item = step * groups + k
            p = item // (local // 4)
            e0 = (item % (local // 4)) * 4
            for w in range(2):
                even = turned[k, pl.ds(64 * w, 32, stride=2), :]
                odd = turned[k, pl.ds(64 * w + 1, 32, stride=2), :]
                mirror_out[p, e0 + w] = jnp.where(low_lanes, even, pltpu.roll(odd, 64, 1))
                mirror_out[p, e0 + 2 + w] = jnp.where(low_lanes, pltpu.roll(even, 64, 1), odd)

    factor = 1.0 / (2 * energies * math.sqrt(energies))

    def put(column, re, im):
        hi, lo = split(re)
        y_hi[:half, column : column + 128] = hi
        y_lo[:half, column : column + 128] = lo
        hi, lo = split(im)
        y_hi[half:, column : column + 128] = hi
        y_lo[half:, column : column + 128] = lo

    def front(buf, h, base, sign):
        re0, re1 = buf[h, 0, :half], buf[h, 0, half:]
        im0, im1 = sign * buf[h, 1, :half], sign * buf[h, 1, half:]
        put(base, re0 + re1, im0 + im1)
        for q, re, im in (
            (1, re0 + im1, im0 - re1),
            (2, re0 - re1, im0 - im1),
            (3, re0 - im1, im0 + re1),
        ):
            c, s = tw[q - 1, 0], tw[q - 1, 1]
            put(base + 128 * q, re * c - im * s, re * s + im * c)

    def dots(rows, hi, lo, columns):
        dot = functools.partial(jnp.dot, preferred_element_type=F32)
        high, low = dft[0, rows], dft[1, rows]
        return dot(high, hi[:, columns]) + dot(high, lo[:, columns]) + dot(low, hi[:, columns])

    def wait_l(h):
        @pl.loop(1, n_energy)
        def _(m):
            l_copy(h, e, (e + n_energy - m) % n_energy).wait_recv()

        l_own(h).wait()

    def wait_g(h):
        @pl.loop(0, n_energy)
        def _(m):
            frm = (e + n_energy - m) % n_energy
            pltpu.make_async_copy(
                mirror_out.at[:, :, 0], g_buf.at[h, :, pl.ds(pl.multiple_of(frm * local, local), local)], g_recv.at[h, frm]
            ).wait()

    def compute_l(h):
        front(l_buf, h, 0, 1.0)
        for c in range(2):
            columns = slice(256 * c, 256 * c + 256)
            spec[:, columns] = dots(slice(None), y_hi, y_lo, columns)

    def compute_g(h):
        front(g_buf, h, 512, -1.0)
        for c in range(2, 4):
            columns = slice(256 * c, 256 * c + 256)
            spec[:, columns] = dots(slice(None), y_hi, y_lo, columns)
        for c in range(4):
            one, two = slice(128 * c, 128 * c + 128), slice(512 + 128 * c, 640 + 128 * c)
            ar, ai = spec[:half, one], spec[half:, one]
            br, bi = spec[:half, two], spec[half:, two]
            hi, lo = split(ar * br + ai * bi)
            v_hi[:half, one] = hi
            v_lo[:half, one] = lo
            hi, lo = split(ar * bi - ai * br)
            v_hi[half:, one] = hi
            v_lo[half:, one] = lo

    def finish(h, part):
        blocks = [slice(local * (2 * k + part), local * (2 * k + part) + local) for k in range(n_energy // 4)]
        later = [slice(half + b.start, half + b.stop) for b in blocks]
        take = lambda ref, index, rows: jnp.concatenate([ref[(*index, r)] for r in rows])
        count = half // 2
        for c in range(2):
            columns = slice(256 * c, 256 * c + 256)
            for rows, to in ((blocks, slice(0, count)), (later, slice(count, half))):
                dot = functools.partial(jnp.dot, preferred_element_type=F32)
                high, low = take(dft, (0,), rows), take(dft, (1,), rows)
                back[to, columns] = (
                    dot(high, v_hi[:, columns]) + dot(high, v_lo[:, columns]) + dot(low, v_hi[:, columns])
                )
        terms = [(back[:count, :128], back[count:half, :128])]
        for q in (1, 2, 3):
            re, im = back[:count, 128 * q : 128 * q + 128], back[count:half, 128 * q : 128 * q + 128]
            c, s = take(tw, (q - 1, 0), blocks), take(tw, (q - 1, 1), blocks)
            terms.append((re * c - im * s, re * s + im * c))
        (r0, i0), (r1, i1), (r2, i2), (r3, i3) = terms
        values = (
            (0, blocks, i0 + i1 + i2 + i3),
            (1, blocks, r0 + r1 + r2 + r3),
            (0, later, i0 - r1 - i2 + r3),
            (1, later, r0 + i1 - r2 - i3),
        )
        for p, rows, value in values:
            for k, r in enumerate(rows):
                p_buf[h, p, r] = value[local * k : local * k + local] * -factor

    def send_p(h, part):
        @pl.loop(0, group)
        def _(m):
            to = 2 * ((e // 2 + m) % group) + part

            @pl.when(to != e)
            def _():
                p_copy(h, to, e).start()

            @pl.when(to == e)
            def _():
                p_own(h).start()

    def drain_l(h):
        @pl.loop(1, n_energy)
        def _(m):
            l_copy(h, (e + m) % n_energy, e).wait_send()

    def drain_g(h):
        @pl.loop(1, n_energy)
        def _(m):
            g_copy(h, (e + m) % n_energy, e).wait_send()

        @pl.when(off_diagonal)
        def _():
            g_copy(h, e, e).wait_send()

        @pl.loop(0, group)
        def _(m):
            for k in range(2):

                @pl.when(handed(k, m))
                def _():
                    second_leg(h, k, m).wait_send()

    def drain_p(h):
        @pl.loop(1, n_energy)
        def _(m):
            to = (e + m) % n_energy
            p_copy(h, to, e).wait_send()
            p_copy(h, e, to).wait_recv()

        p_own(h).wait()

    signals = n_energy - 1 + jnp.where(off_diagonal, n_energy, 0)
    signals -= jnp.where(kind == HALF, group, 0) + jnp.where(kind == ROUND, n_energy // 4, 0)
    for how in (kind, hands):
        signals += jnp.where(how > 0, 1, 0)
    for how in (hands, gets):
        signals += jnp.where(how == HALF, group, 0) + jnp.where(how == ROUND, n_energy // 4, 0)
    pl.semaphore_wait(barrier, signals)

    for h in range(2):
        send_legs(h)
        send_g(h)
        send_l(h)
        if h == 0:
            hand_on(h)
    load_dft.wait()
    load_tw.wait()

    def spectrum(h):
        wait_l(h)
        compute_l(h)

    def rest(h):
        wait_g(h)
        compute_g(h)
        for part in range(2):
            finish(h, part)
            send_p(h, part)

    spectrum(0)
    hand_on(1)
    rest(0)
    spectrum(1)
    rest(1)

    @pl.loop(0, 2)
    def _(h):
        drain_l(h)
        drain_g(h)
        drain_p(h)


def on_device(lesser, greater):
    n_energy = lax.axis_size("energy")
    side = math.isqrt(lax.axis_size("tile"))
    local, cells = lesser.shape[1], lesser.shape[3]
    rows = cells // 128
    energies = n_energy * local
    dft, twiddle = tables(energies, 128)
    any_space = pl.BlockSpec(memory_space=pltpu.HBM)
    half = energies // 2
    out = pl.pallas_call(
        functools.partial(body, n_energy, side),
        out_shape=jax.ShapeDtypeStruct((2, local, rows, 128), F32),
        in_specs=[any_space] * 4,
        out_specs=any_space,
        scratch_shapes=[
            pltpu.VMEM((2, local, rows, 128), F32),
            pltpu.VMEM((4, 128, 128), F32),
            pltpu.VMEM((4, 128, 128), F32),
            pltpu.VMEM((2, local, rows, 128), F32),
            pltpu.VMEM((2, 2, energies, 128), F32),
            pltpu.VMEM((2, 2, energies, 128), F32),
            pltpu.VMEM((2, 2, energies, 128), F32),
            pltpu.VMEM((2, 2, n_energy // 2, 2, local, 128), F32),
            pltpu.VMEM((2, energies, energies), BF),
            pltpu.VMEM((3, 2, half, 128), F32),
            pltpu.VMEM((energies, 1024), BF),
            pltpu.VMEM((energies, 1024), BF),
            pltpu.VMEM((energies, 1024), F32),
            pltpu.VMEM((energies, 512), BF),
            pltpu.VMEM((energies, 512), BF),
            pltpu.VMEM((energies, 512), F32),
            pltpu.SemaphoreType.DMA((3,)),
            pltpu.SemaphoreType.DMA((2,)),
        ]
        + [pltpu.SemaphoreType.DMA((2, n_energy))] * 6
        + [pltpu.SemaphoreType.DMA((2, 2, n_energy // 2))] * 2,
        compiler_params=pltpu.CompilerParams(
            collective_id=0, has_side_effects=True, vmem_limit_bytes=40 * 2**20
        ),
        name="correlate",
    )(
        pltpu.with_memory_space_constraint(lesser.reshape(2, local, rows, 128), pltpu.HBM),
        pltpu.with_memory_space_constraint(greater.reshape(2, local, rows, 128), pltpu.HBM),
        pltpu.with_memory_space_constraint(jnp.asarray(dft), pltpu.HBM),
        pltpu.with_memory_space_constraint(jnp.asarray(twiddle), pltpu.HBM),
    )
    return out.reshape(2, local, 1, cells)


def solution(mesh):
    return jax.shard_map(
        on_device,
        mesh=mesh,
        in_specs=(P(None, "energy", "tile", None), P(None, "energy", "tile", None)),
        out_specs=P(None, "energy", "tile", None),
        check_vma=False,
    )
```

```python
import functools
import math

import jax
import jax.numpy as jnp
import ml_dtypes
import numpy as np
from jax import lax
from jax.experimental import pallas as pl
from jax.experimental.pallas import tpu as pltpu
from jax.sharding import PartitionSpec as P

MESH = pl.DeviceIdType.MESH
BF = jnp.bfloat16
F32 = jnp.float32


def tables(energies, lanes):
    length = 2 * energies
    quarter = length // 4
    n = np.arange(quarter)
    angle = 2.0 * np.pi * (np.outer(n, n) % quarter) / quarter
    cos, sin = np.cos(angle), np.sin(angle)
    full = np.block([[cos, sin], [-sin, cos]]).astype(np.float32)
    high = full.astype(ml_dtypes.bfloat16)
    low = (full - high.astype(np.float32)).astype(ml_dtypes.bfloat16)
    rows = []
    for q in (1, 2, 3):
        turn = 2.0 * np.pi * ((n * q) % length) / length
        rows.append(np.stack([np.cos(turn), -np.sin(turn)]))
    twiddle = np.stack(rows).astype(np.float32)
    twiddle = np.ascontiguousarray(np.broadcast_to(twiddle[..., None], twiddle.shape + (lanes,)))
    return np.stack([high, low]), twiddle


HALF, ROUND = 1, 2
KINDS = tuple((k, HALF) for k in (2, 3, 6, 7, 8, 9, 12, 13)) + tuple((k, ROUND) for k in (1, 4, 11, 14))
ROUND_BY = ((1, 7), (4, 6), (11, 9), (14, 8))


def pick(key, table):
    value = jnp.int32(0)
    for k, v in table:
        value = jnp.where(key == k, jnp.int32(v), value)
    return value


def split(x):
    high = x.astype(BF)
    return high, (x - high.astype(F32)).astype(BF)


def body(
    n_energy, side, lesser, greater, dft_hbm, tw_hbm, out,
    g_in, stage, turned, mirror_out, l_buf, g_buf, p_buf, held, dft, tw, y_hi, y_lo, spec, v_hi, v_lo, back,
    in_sem, own_sem, l_send, g_send, p_send, l_recv, g_recv, p_recv, r_recv, f_send,
):
    e = lax.axis_index("energy")
    t = lax.axis_index("tile")
    t2 = (t % side) * side + t // side
    off_diagonal = t2 != t
    local = g_in.shape[1]
    energies = n_energy * local
    half = energies // 2

    load_g = pltpu.make_async_copy(greater, g_in, in_sem.at[0])
    load_g.start()
    load_dft = pltpu.make_async_copy(dft_hbm, dft, in_sem.at[1])
    load_tw = pltpu.make_async_copy(tw_hbm, tw, in_sem.at[2])

    mirror = lambda k: (k % side) * side + k // side
    n_tile = side * side
    group = n_energy // 2
    base = (e // group) * group
    other = (e + group) % n_energy
    across = (t + n_tile // 2) % n_tile
    kind = pick(t, KINDS)
    relay = jnp.where(kind == ROUND, pick(t, ROUND_BY), across)
    round_from = pick(t, [(b, a) for a, b in ROUND_BY])
    source = jnp.where(round_from > 0, round_from, across)
    hands = pick(source, KINDS)
    hands = jnp.where(jnp.logical_and(hands == ROUND, round_from == 0), 0, hands)
    final = mirror(source)
    gets = pick(t2, KINDS)
    last = jnp.where(gets == ROUND, pick(t2, ROUND_BY), (t2 + n_tile // 2) % n_tile)

    def by_relay(how, frm, to):
        same = to // group == frm // group
        return jnp.logical_or(
            jnp.logical_and(how == HALF, same), jnp.logical_and(how == ROUND, (to + frm) % 4 == 0)
        )

    fourth = lambda m: 4 * m + (n_energy - e) % 4

    barrier = pltpu.get_barrier_semaphore()

    def greet(to, tile):
        pl.semaphore_signal(barrier, inc=1, device_id=(to, tile), device_id_type=MESH)

    @pl.loop(1, n_energy)
    def _(m):
        greet((e + m) % n_energy, t)

    @pl.when(off_diagonal)
    def _():
        @pl.loop(0, n_energy)
        def _(m):
            to = (e + m) % n_energy

            @pl.when(jnp.logical_not(by_relay(kind, e, to)))
            def _():
                greet(to, t2)

    def greet_relay(how, tile):
        @pl.when(how > 0)
        def _():
            greet(e, tile)

    def greet_group(how, tile):
        @pl.when(how == HALF)
        def _():
            @pl.loop(0, group)
            def _(m):
                greet(base + m, tile)

        @pl.when(how == ROUND)
        def _():
            @pl.loop(0, n_energy // 4)
            def _(m):
                greet(fourth(m), tile)

    greet_relay(kind, relay)
    greet_relay(hands, source)
    greet_group(hands, final)
    greet_group(gets, last)

    def l_copy(h, to, frm):
        return pltpu.make_async_remote_copy(
            src_ref=lesser.at[:, :, h * n_energy + to],
            dst_ref=l_buf.at[h, :, pl.ds(pl.multiple_of(frm * local, local), local)],
            send_sem=l_send.at[h, to],
            recv_sem=l_recv.at[h, frm],
            device_id=(to, t),
            device_id_type=MESH,
        )

    def g_copy(h, to, frm):
        return pltpu.make_async_remote_copy(
            src_ref=mirror_out.at[:, :, h * n_energy + to],
            dst_ref=g_buf.at[h, :, pl.ds(pl.multiple_of(frm * local, local), local)],
            send_sem=g_send.at[h, to],
            recv_sem=g_recv.at[h, frm],
            device_id=(to, t2),
            device_id_type=MESH,
        )

    def first_leg(h, to):
        return pltpu.make_async_remote_copy(
            src_ref=mirror_out.at[:, :, h * n_energy + to],
            dst_ref=held.at[h, jnp.where(to // group == e // group, 0, 1), to % group],
            send_sem=g_send.at[h, to],
            recv_sem=r_recv.at[h, jnp.where(to // group == e // group, 0, 1), to % group],
            device_id=(jnp.where(kind == ROUND, e, (to // group) * group + e % group), relay),
            device_id_type=MESH,
        )

    def second_leg(h, k, m):
        frm = e if k == 0 else jnp.where(hands == ROUND, e, other)
        to = base + m if k == 0 else jnp.where(hands == ROUND, (base + group) % n_energy, base) + m
        return pltpu.make_async_remote_copy(
            src_ref=held.at[h, k, m],
            dst_ref=g_buf.at[h, :, pl.ds(pl.multiple_of(frm * local, local), local)],
            send_sem=f_send.at[h, k, m],
            recv_sem=g_recv.at[h, frm],
            device_id=(to, final),
            device_id_type=MESH,
        )

    def handed(k, m):
        quarter = jnp.logical_and(hands == ROUND, (m + e) % 4 == 0)
        return jnp.logical_or(hands == HALF, quarter) if k == 0 else quarter

    def p_copy(h, to, frm):
        return pltpu.make_async_remote_copy(
            src_ref=p_buf.at[h, :, pl.ds(pl.multiple_of(to * local, local), local)],
            dst_ref=out.at[:, :, h * n_energy + frm],
            send_sem=p_send.at[h, to],
            recv_sem=p_recv.at[h, frm],
            device_id=(to, t),
            device_id_type=MESH,
        )

    def l_own(h):
        return pltpu.make_async_copy(
            lesser.at[:, :, h * n_energy + e], l_buf.at[h, :, pl.ds(pl.multiple_of(e * local, local), local)], l_recv.at[h, e]
        )

    def g_own(h):
        return pltpu.make_async_copy(
            mirror_out.at[:, :, h * n_energy + e], g_buf.at[h, :, pl.ds(pl.multiple_of(e * local, local), local)], g_recv.at[h, e]
        )

    def p_own(h):
        return pltpu.make_async_copy(
            p_buf.at[h, :, pl.ds(pl.multiple_of(e * local, local), local)], out.at[:, :, h * n_energy + e], p_recv.at[h, e]
        )

    def send_l(h):
        @pl.loop(1, n_energy)
        def _(m):
            l_copy(h, (e + m) % n_energy, e).start()

        l_own(h).start()

    def send_legs(h):
        @pl.when(kind == ROUND)
        def _():
            @pl.loop(0, n_energy // 4)
            def _(m):
                first_leg(h, fourth(m)).start()

        @pl.when(kind == HALF)
        def _():
            @pl.loop(0, group)
            def _(m):
                first_leg(h, base + (e + m) % group).start()

    def send_g(h):
        @pl.loop(0, group)
        def _(m):
            for start in (base, (base + group) % n_energy):
                to = start + (e + m) % group
                own = jnp.logical_and(to == e, jnp.logical_not(off_diagonal))

                @pl.when(jnp.logical_not(jnp.logical_or(by_relay(kind, e, to), own)))
                def _():
                    g_copy(h, to, e).start()

        @pl.when(jnp.logical_not(off_diagonal))
        def _():
            g_own(h).start()

    def hand_on(h):
        @pl.loop(0, group)
        def _(step):
            m = (e + step) % group
            for k in range(2):

                @pl.when(handed(k, m))
                def _():
                    pltpu.make_async_copy(mirror_out.at[:, :, 0], held.at[h, k, m], r_recv.at[h, k, m]).wait()
                    second_leg(h, k, m).start()

    load_dft.start()
    load_tw.start()
    load_g.wait()

    low_lanes = lax.broadcasted_iota(jnp.int32, (32, 128), 1) < 64

    groups = stage.shape[0]

    @pl.loop(0, 2 * local // (4 * groups))
    def _(step):
        for k in range(groups):
            item = step * groups + k
            p = item // (local // 4)
            e0 = (item % (local // 4)) * 4
            for q in range(2):
                one = g_in[p, e0 + 2 * q]
                two = g_in[p, e0 + 2 * q + 1]
                stage[k, pl.ds(64 * q, 32, stride=2), :] = jnp.where(low_lanes, one, pltpu.roll(two, 64, 1))
                stage[k, pl.ds(64 * q + 1, 32, stride=2), :] = jnp.where(low_lanes, pltpu.roll(one, 64, 1), two)
        for k in range(groups):
            turned[k] = stage[k].T
        for k in range(groups):
            item = step * groups + k
            p = item // (local // 4)
            e0 = (item % (local // 4)) * 4
            for w in range(2):
                even = turned[k, pl.ds(64 * w, 32, stride=2), :]
                odd = turned[k, pl.ds(64 * w + 1, 32, stride=2), :]
                mirror_out[p, e0 + w] = jnp.where(low_lanes, even, pltpu.roll(odd, 64, 1))
                mirror_out[p, e0 + 2 + w] = jnp.where(low_lanes, pltpu.roll(even, 64, 1), odd)

    factor = 1.0 / (2 * energies * math.sqrt(energies))

    def put(column, re, im):
        hi, lo = split(re)
        y_hi[:half, column : column + 128] = hi
        y_lo[:half, column : column + 128] = lo
        hi, lo = split(im)
        y_hi[half:, column : column + 128] = hi
        y_lo[half:, column : column + 128] = lo

    def front(buf, h, base, sign):
        re0, re1 = buf[h, 0, :half], buf[h, 0, half:]
        im0, im1 = sign * buf[h, 1, :half], sign * buf[h, 1, half:]
        put(base, re0 + re1, im0 + im1)
        for q, re, im in (
            (1, re0 + im1, im0 - re1),
            (2, re0 - re1, im0 - im1),
            (3, re0 - im1, im0 + re1),
        ):
            c, s = tw[q - 1, 0], tw[q - 1, 1]
            put(base + 128 * q, re * c - im * s, re * s + im * c)

    def dots(rows, hi, lo, columns):
        dot = functools.partial(jnp.dot, preferred_element_type=F32)
        high, low = dft[0, rows], dft[1, rows]
        return dot(high, hi[:, columns]) + dot(high, lo[:, columns]) + dot(low, hi[:, columns])

    def wait_l(h):
        @pl.loop(1, n_energy)
        def _(m):
            l_copy(h, e, (e + n_energy - m) % n_energy).wait_recv()

        l_own(h).wait()

    def wait_g(h):
        @pl.loop(0, n_energy)
        def _(m):
            frm = (e + n_energy - m) % n_energy
            pltpu.make_async_copy(
                mirror_out.at[:, :, 0], g_buf.at[h, :, pl.ds(pl.multiple_of(frm * local, local), local)], g_recv.at[h, frm]
            ).wait()

    def compute_l(h):
        front(l_buf, h, 0, 1.0)
        for c in range(2):
            columns = slice(256 * c, 256 * c + 256)
            spec[:, columns] = dots(slice(None), y_hi, y_lo, columns)

    def compute_g(h):
        front(g_buf, h, 512, -1.0)
        for c in range(2, 4):
            columns = slice(256 * c, 256 * c + 256)
            spec[:, columns] = dots(slice(None), y_hi, y_lo, columns)
        for c in range(4):
            one, two = slice(128 * c, 128 * c + 128), slice(512 + 128 * c, 640 + 128 * c)
            ar, ai = spec[:half, one], spec[half:, one]
            br, bi = spec[:half, two], spec[half:, two]
            hi, lo = split(ar * br + ai * bi)
            v_hi[:half, one] = hi
            v_lo[:half, one] = lo
            hi, lo = split(ar * bi - ai * br)
            v_hi[half:, one] = hi
            v_lo[half:, one] = lo

    def finish(h, part):
        blocks = [slice(local * (2 * k + part), local * (2 * k + part) + local) for k in range(n_energy // 4)]
        later = [slice(half + b.start, half + b.stop) for b in blocks]
        take = lambda ref, index, rows: jnp.concatenate([ref[(*index, r)] for r in rows])
        count = half // 2
        for c in range(2):
            columns = slice(256 * c, 256 * c + 256)
            for rows, to in ((blocks, slice(0, count)), (later, slice(count, half))):
                dot = functools.partial(jnp.dot, preferred_element_type=F32)
                high, low = take(dft, (0,), rows), take(dft, (1,), rows)
                back[to, columns] = (
                    dot(high, v_hi[:, columns]) + dot(high, v_lo[:, columns]) + dot(low, v_hi[:, columns])
                )
        terms = [(back[:count, :128], back[count:half, :128])]
        for q in (1, 2, 3):
            re, im = back[:count, 128 * q : 128 * q + 128], back[count:half, 128 * q : 128 * q + 128]
            c, s = take(tw, (q - 1, 0), blocks), take(tw, (q - 1, 1), blocks)
            terms.append((re * c - im * s, re * s + im * c))
        (r0, i0), (r1, i1), (r2, i2), (r3, i3) = terms
        values = (
            (0, blocks, i0 + i1 + i2 + i3),
            (1, blocks, r0 + r1 + r2 + r3),
            (0, later, i0 - r1 - i2 + r3),
            (1, later, r0 + i1 - r2 - i3),
        )
        for p, rows, value in values:
            for k, r in enumerate(rows):
                p_buf[h, p, r] = value[local * k : local * k + local] * -factor

    def send_p(h, part):
        @pl.loop(0, group)
        def _(m):
            to = 2 * ((e // 2 + m) % group) + part

            @pl.when(to != e)
            def _():
                p_copy(h, to, e).start()

            @pl.when(to == e)
            def _():
                p_own(h).start()

    def drain_l(h):
        @pl.loop(1, n_energy)
        def _(m):
            l_copy(h, (e + m) % n_energy, e).wait_send()

    def drain_g(h):
        @pl.loop(1, n_energy)
        def _(m):
            g_copy(h, (e + m) % n_energy, e).wait_send()

        @pl.when(off_diagonal)
        def _():
            g_copy(h, e, e).wait_send()

        @pl.loop(0, group)
        def _(m):
            for k in range(2):

                @pl.when(handed(k, m))
                def _():
                    second_leg(h, k, m).wait_send()

    def drain_p(h):
        @pl.loop(1, n_energy)
        def _(m):
            to = (e + m) % n_energy
            p_copy(h, to, e).wait_send()
            p_copy(h, e, to).wait_recv()

        p_own(h).wait()

    signals = n_energy - 1 + jnp.where(off_diagonal, n_energy, 0)
    signals -= jnp.where(kind == HALF, group, 0) + jnp.where(kind == ROUND, n_energy // 4, 0)
    for how in (kind, hands):
        signals += jnp.where(how > 0, 1, 0)
    for how in (hands, gets):
        signals += jnp.where(how == HALF, group, 0) + jnp.where(how == ROUND, n_energy // 4, 0)
    pl.semaphore_wait(barrier, signals)

    send_legs(0)
    send_g(0)
    send_l(0)
    hand_on(0)
    send_legs(1)
    send_g(1)
    load_dft.wait()
    load_tw.wait()

    def spectrum(h):
        wait_l(h)
        compute_l(h)

    def rest(h):
        wait_g(h)
        compute_g(h)
        for part in range(2):
            finish(h, part)
            send_p(h, part)

    spectrum(0)
    hand_on(1)
    send_l(1)
    rest(0)
    spectrum(1)
    rest(1)

    @pl.loop(0, 2)
    def _(h):
        drain_l(h)
        drain_g(h)
        drain_p(h)


def on_device(lesser, greater):
    n_energy = lax.axis_size("energy")
    side = math.isqrt(lax.axis_size("tile"))
    local, cells = lesser.shape[1], lesser.shape[3]
    rows = cells // 128
    energies = n_energy * local
    dft, twiddle = tables(energies, 128)
    any_space = pl.BlockSpec(memory_space=pltpu.HBM)
    half = energies // 2
    out = pl.pallas_call(
        functools.partial(body, n_energy, side),
        out_shape=jax.ShapeDtypeStruct((2, local, rows, 128), F32),
        in_specs=[any_space] * 4,
        out_specs=any_space,
        scratch_shapes=[
            pltpu.VMEM((2, local, rows, 128), F32),
            pltpu.VMEM((4, 128, 128), F32),
            pltpu.VMEM((4, 128, 128), F32),
            pltpu.VMEM((2, local, rows, 128), F32),
            pltpu.VMEM((2, 2, energies, 128), F32),
            pltpu.VMEM((2, 2, energies, 128), F32),
            pltpu.VMEM((2, 2, energies, 128), F32),
            pltpu.VMEM((2, 2, n_energy // 2, 2, local, 128), F32),
            pltpu.VMEM((2, energies, energies), BF),
            pltpu.VMEM((3, 2, half, 128), F32),
            pltpu.VMEM((energies, 1024), BF),
            pltpu.VMEM((energies, 1024), BF),
            pltpu.VMEM((energies, 1024), F32),
            pltpu.VMEM((energies, 512), BF),
            pltpu.VMEM((energies, 512), BF),
            pltpu.VMEM((energies, 512), F32),
            pltpu.SemaphoreType.DMA((3,)),
            pltpu.SemaphoreType.DMA((2,)),
        ]
        + [pltpu.SemaphoreType.DMA((2, n_energy))] * 6
        + [pltpu.SemaphoreType.DMA((2, 2, n_energy // 2))] * 2,
        compiler_params=pltpu.CompilerParams(
            collective_id=0, has_side_effects=True, vmem_limit_bytes=40 * 2**20
        ),
        name="correlate",
    )(
        pltpu.with_memory_space_constraint(lesser.reshape(2, local, rows, 128), pltpu.HBM),
        pltpu.with_memory_space_constraint(greater.reshape(2, local, rows, 128), pltpu.HBM),
        pltpu.with_memory_space_constraint(jnp.asarray(dft), pltpu.HBM),
        pltpu.with_memory_space_constraint(jnp.asarray(twiddle), pltpu.HBM),
    )
    return out.reshape(2, local, 1, cells)


def solution(mesh):
    return jax.shard_map(
        on_device,
        mesh=mesh,
        in_specs=(P(None, "energy", "tile", None), P(None, "energy", "tile", None)),
        out_specs=P(None, "energy", "tile", None),
        check_vma=False,
    )
```
